512 devices in a mesh: ctx: 8 (over y, core), exp: 64 (over z, x).
Axes of the slice: x: 4, y: 4, z: 16, core: 2. Of those that a mesh axis runs over, the one named last changes fastest.
Arguments:
- prefill_cache: bfloat16 [512, 512, 576], P('ctx', 'exp'), may hold values from -600 to 600
- owner_slot: int32 [512], replicated, may hold values from 0 to 511, as said below
- cached_len: int32 [512], replicated, may hold values from 1 to 512
- query_latent: bfloat16 [512, 1536], P('ctx'), may hold values from -6 to 6
- new_latent: bfloat16 [512, 576], P('ctx'), may hold values from -6 to 6
- wq_up: bfloat16 [1536, 64, 192], P(None, 'exp'), may hold values from -0.15625 to 0.15625
- wk_up: bfloat16 [64, 128, 512], P('exp'), may hold values from -0.5 to 0.5
- wv_up: bfloat16 [64, 512, 128], P('exp'), may hold values from -0.25 to 0.25
- w_out: bfloat16 [8192, 7168], P('exp'), may hold values from -0.0625 to 0.0625
- residual: bfloat16 [512, 7168], P(('ctx', 'exp')), may hold values from -6 to 6
- ffn_gain: float32 [7168], replicated, may hold values from 0.5 to 1.5
- expert_ids: int32 [512, 8], P('ctx'), may hold values from 0 to 255, all different within a row; in each aligned block of 64 rows (0 to 63, 64 to 127, ...) at most 4 rows name the same one
Outputs:
- hidden_out: bfloat16 [512, 7168], P(('ctx', 'exp'))
- expert_in: bfloat16 [8, 256, 4, 7168], P('ctx', 'exp')
The draws below stay inside these ranges and needn't reach their ends.
Inputs may be any that keep to these rules, and one draw needn't show every extreme that they name: A permutation of decode rows; request r goes to owner owner_slot[r] // 64. The 64 requests of one prefill shard (r // 64 equal) send at most 16 to one owner, and some shard sends exactly 16 to some owner. `expert_ids`: in each aligned block of 64 rows (one owner) no expert is chosen by more than 4 rows.
All inputs are finite; a program needn't handle non-finite values.
Results may differ from the reference program's by a relative error of at most 0.008.
Values may be sent and summed in bfloat16 or wider, within the bound.
A program may use at most 64 MiB of HBM per device.

```python
import math
import jax
import jax.numpy as jnp
import numpy as np
from jax import lax

D = 7168
QL = 1536
KVL = 512
RD = 64
NOPE = 128
VD = 128
H = 64
EXPERTS = 256
TOPK = 8
CAP = 4
ROWS = 64
LLOC = 8
CACHE = 512
LAT = 576
DEC = 512
N_CTX = 8
N_EXP = 64


def draw_prefill_cache(key, part):
    key = jax.random.fold_in(key, 37)
    key_base = jax.random.fold_in(key, 0)
    latents = jnp.clip(jax.random.normal(key_base, (DEC, CACHE, LAT), jnp.float32), -6.0, 6.0)
    return latents.astype(jnp.bfloat16)


def draw_owner_slot(key, part):
    key = jax.random.fold_in(key, 11)
    key_cycle, key_order, key_place = jax.random.split(key, 3)
    total = N_CTX * ROWS
    base = ROWS // N_CTX
    owners = jnp.arange(N_CTX, dtype=jnp.int32)
    sigma = jax.random.permutation(key_cycle, N_CTX).astype(jnp.int32)
    counts = base + base * (owners[None, :] == sigma[:, None]).astype(jnp.int32) - base * (owners[None, :] == jnp.roll(sigma, -1)[:, None]).astype(jnp.int32)
    bounds = jnp.cumsum(counts, axis=1)
    places = jnp.arange(ROWS, dtype=jnp.int32)
    sorted_dest = jnp.sum((bounds[:, None, :] <= places[None, :, None]).astype(jnp.int32), 2)
    orders = jax.vmap(lambda sub: jax.random.permutation(sub, ROWS))(jax.random.split(key_order, N_CTX))
    dest = jnp.take_along_axis(sorted_dest, orders.astype(jnp.int32), axis=1).reshape(total)
    onehot = (dest[:, None] == owners[None, :]).astype(jnp.int32)
    ranks = jnp.sum((jnp.cumsum(onehot, 0) - onehot) * onehot, 1)
    spots = jax.vmap(lambda sub: jax.random.permutation(sub, ROWS))(jax.random.split(key_place, N_CTX)).astype(jnp.int32)
    return (dest * ROWS + spots[dest, ranks]).astype(jnp.int32)


def draw_cached_len(key, part):
    key = jax.random.fold_in(key, 23)
    key_len, key_pick = jax.random.split(key)
    total = N_CTX * ROWS
    lengths = jax.random.randint(key_len, (total,), 1, CACHE + 1, dtype=jnp.int32)
    chosen = jax.random.randint(key_pick, (), 0, total, dtype=jnp.int32)
    return lengths.at[chosen].set(CACHE).astype(jnp.int32)


def steps_of(own_key, extent, cuts, low, top_value):
    def one(dim, blocks):
        heights = jax.random.uniform(jax.random.fold_in(jax.random.fold_in(own_key, 6), dim), (blocks,), jnp.float32, low / len(cuts), top_value / len(cuts))
        return jnp.repeat(jnp.exp(heights), extent[dim] // blocks).reshape((-1,) + (1,) * (len(extent) - dim - 1))

    factor_of = one(*cuts[0])
    for cut in cuts[1:]:
        factor_of = factor_of * one(*cut)
    return factor_of


def assign_block(key, own, number, rows, number_of, top, bound, slope):
    order = jax.random.permutation(key, number_of)
    packed, ordinary = portions_of(number_of, rows * top, bound, slope, True), portions_of(number_of, rows * top, bound, slope, False)
    places = jnp.arange(number_of)

    def named(sizes, offset_by):
        used = int((sizes > 0).sum())
        fixed = max(1, used // 4)
        shifted = fixed + (places - fixed + offset_by * (used - fixed)) % max(1, number_of - fixed)
        return jnp.zeros((number_of,), jnp.int32).at[order[jnp.where(places < fixed, places, shifted)]].set(jnp.asarray(sizes, jnp.int32))

    sizes = jnp.where(number % 4 == 0, named(packed, number // 4), named(ordinary, number - number // 4 - 1))
    mixed = jax.random.permutation(jax.random.fold_in(own, 3), number_of)
    giver, receiver = mixed[0:number_of // 2 * 2:2], mixed[1:number_of // 2 * 2:2]
    room = jnp.minimum(sizes[giver] - 1, bound - sizes[receiver]) // 2
    room = jnp.where((giver == order[0]) | (receiver == order[0]) | (sizes[receiver] == 0), 0, jnp.maximum(room, 0))
    shifted = jax.random.randint(jax.random.fold_in(own, 4), (number_of // 2,), 0, 1 << 20) % (room + 1)
    sizes = sizes.at[giver].add(-shifted).at[receiver].add(shifted)
    items = jnp.searchsorted(jnp.cumsum(sizes), jnp.arange(rows * top), side="right").astype(jnp.int32)
    grid = items.reshape(top, rows).T
    grid = grid[jax.random.permutation(jax.random.fold_in(own, 1), rows)]
    offset_by = jax.random.randint(jax.random.fold_in(own, 2), (rows, 1), 0, top)
    return jnp.take_along_axis(grid, (jnp.arange(top)[None, :] + offset_by) % top, axis=1)


def portions_of(amount, total, reach, skew, full):
    weights = [(1 << 20) // math.isqrt(standing ** skew) + 1 for standing in range(1, amount + 1)]
    largest = reach if full else min(reach, max(-(-total // amount), total * weights[0] // sum(weights)))
    least = 1 if total - largest >= amount - 1 else 0
    holding, rest = [largest] + [least] * (amount - 1), total - largest - least * (amount - 1)
    while rest > 0:
        free = [i for i in range(1, amount) if holding[i] < largest] or [i for i in range(1, amount) if holding[i] < reach]
        mass, left = sum([weights[i] for i in free]), rest
        for i in free:
            more = min(reach - holding[i], max(1, left * weights[i] // mass), rest)
            holding[i] = holding[i] + more
            rest = rest - more
    return np.array(holding)


def normal_values(rng, shape, scale, most, shards=(), kind=jnp.bfloat16):
    gain = steps_of(rng, shape, shards, -0.22, 0.18) if shards else 1.0
    values = jax.random.normal(rng, shape, jnp.float32) * scale * gain
    return jnp.minimum(jnp.maximum(values, -most), most).astype(kind)


def setup_inputs(seed: int = 0) -> dict:
    seeds = jax.random.split(jax.random.key(seed), 13)
    prefill_cache = draw_prefill_cache(jax.random.fold_in(seeds[12], 71), 0)
    owner_slot = draw_owner_slot(jax.random.fold_in(seeds[12], 71), 0)
    cached_len = draw_cached_len(jax.random.fold_in(seeds[12], 71), 0)
    query_latent = normal_values(seeds[3], (DEC, QL), 1.0, 6.0, ((0, 8),))
    new_latent = normal_values(seeds[4], (DEC, LAT), 1.0, 6.0, ((0, 8),))
    wq_up = normal_values(seeds[5], (QL, H, NOPE + RD), QL ** -0.5, 0.15625, ((1, 64),))
    wk_up = normal_values(seeds[6], (H, NOPE, KVL), NOPE ** -0.5, 0.5, ((0, 64),))
    wv_up = normal_values(seeds[7], (H, KVL, VD), KVL ** -0.5, 0.25, ((0, 64),))
    w_out = normal_values(seeds[8], (H * VD, D), (H * VD) ** -0.5, 0.0625, ((0, 64),))
    residual = normal_values(seeds[9], (DEC, D), 1.0, 6.0, ((0, 512),))
    ffn_gain = jnp.clip(1.0 + 0.1 * jax.random.normal(seeds[10], (D,), jnp.float32), 0.5, 1.5)
    expert_ids_keys = jax.random.split(jax.random.fold_in(seeds[11], 1), DEC // ROWS)
    expert_ids_turns = jax.random.permutation(jax.random.fold_in(seeds[11], 3), DEC // ROWS)
    expert_ids = jax.vmap(lambda own, number: assign_block(jax.random.fold_in(seeds[11], 2), own, number, ROWS, EXPERTS, TOPK, CAP, 1))(expert_ids_keys, expert_ids_turns).reshape((DEC, TOPK))
    return {"prefill_cache": prefill_cache, "owner_slot": owner_slot, "cached_len": cached_len, "query_latent": query_latent, "new_latent": new_latent, "wq_up": wq_up, "wk_up": wk_up, "wv_up": wv_up, "w_out": w_out, "residual": residual, "ffn_gain": ffn_gain, "expert_ids": expert_ids}


def rotate(part, positions):
    half = part.shape[-1] // 2
    index = jnp.arange(half, dtype=jnp.float32)
    freqs = 10000.0 ** (-2.0 * index / part.shape[-1])
    angles = positions.astype(jnp.float32)[:, None, None] * freqs
    first = part[..., :half]
    second = part[..., half:]
    return jnp.concatenate([first * jnp.cos(angles) - second * jnp.sin(angles), first * jnp.sin(angles) + second * jnp.cos(angles)], -1)

def normalize(hidden, ffn_gain):
    return (hidden * lax.rsqrt(lax.optimization_barrier(jnp.mean(hidden * hidden, -1, keepdims=True)) + 1e-06) * ffn_gain).astype(jnp.bfloat16)

def reference(prefill_cache, owner_slot, cached_len, query_latent, new_latent, wq_up, wk_up, wv_up, w_out, residual, ffn_gain, expert_ids):
    total = owner_slot.shape[0]
    anchor = jnp.zeros((total,), jnp.int32).at[owner_slot].set(jnp.arange(total, dtype=jnp.int32))
    lengths = cached_len[anchor]
    cache = prefill_cache[anchor]
    q_full = jnp.einsum('rq,qhd->rhd', query_latent.astype(jnp.float32), wq_up.astype(jnp.float32)).astype(jnp.bfloat16)
    q_abs = jnp.einsum('rhn,hnc->rhc', q_full[..., :NOPE].astype(jnp.float32), wk_up.astype(jnp.float32))
    queries = jnp.concatenate([q_abs, rotate(q_full[..., NOPE:].astype(jnp.float32), lengths)], -1).astype(jnp.bfloat16)
    scale = 1.0 / math.sqrt(NOPE + RD)

    def attend(group_args):
        q_group, cache_group, len_group, new_group = group_args
        q_float = q_group.astype(jnp.float32)
        new_scores = jnp.einsum('rhc,rc->rh', q_float, new_group.astype(jnp.float32)) * scale
        new_values = new_group[:, None, :KVL].astype(jnp.float32)

        def shard_terms(block):
            keys = lax.dynamic_slice_in_dim(cache_group, block * LLOC, LLOC, 1).astype(jnp.float32)
            scores = jnp.einsum('rhc,rlc->rhl', q_float, keys) * scale
            position = block * LLOC + jnp.arange(LLOC, dtype=jnp.int32)
            valid = (position[None, :] < len_group[:, None])[:, None, :]
            first = block == 0
            local_max = lax.optimization_barrier(jnp.max(jnp.where(valid, scores, -1e+30), 2))
            top = jnp.where(first, jnp.maximum(local_max, new_scores), local_max)
            weights = jnp.where(valid, jnp.exp(scores - top[..., None]), 0.0)
            new_weight = jnp.where(first, jnp.exp(new_scores - top), 0.0)
            total_weight = lax.optimization_barrier(jnp.sum(weights, 2)) + new_weight
            rounded = lax.optimization_barrier(weights.astype(jnp.bfloat16))
            mixed = jnp.einsum('rhl,rlc->rhc', rounded.astype(jnp.float32), keys[..., :KVL])
            new_rounded = lax.optimization_barrier(new_weight.astype(jnp.bfloat16))
            mixed = (mixed + new_rounded.astype(jnp.float32)[..., None] * new_values).astype(jnp.bfloat16)
            return (top, total_weight, mixed)
        tops, totals = lax.map(lambda block: shard_terms(block)[:2], jnp.arange(N_EXP, dtype=jnp.int32))
        peak = lax.optimization_barrier(jnp.max(tops, 0))

        def accumulate(carry, block):
            top, total_weight, mixed = shard_terms(block)
            factor = jnp.exp(top - peak)
            return ((carry[0] + factor[..., None] * mixed.astype(jnp.float32), carry[1] + factor * total_weight), None)
        start = (jnp.zeros((ROWS, H, KVL), jnp.float32), jnp.zeros((ROWS, H), jnp.float32))
        (numer, denom), _ = lax.scan(accumulate, start, jnp.arange(N_EXP, dtype=jnp.int32))
        return (numer / denom[..., None]).astype(jnp.bfloat16)
    latent_out = lax.map(attend, (queries.reshape(N_CTX, ROWS, H, LAT), cache.reshape(N_CTX, ROWS, CACHE, LAT), lengths.reshape(N_CTX, ROWS), new_latent.reshape(N_CTX, ROWS, LAT))).reshape(total, H, KVL)
    heads_out = jnp.einsum('rhc,hcv->rhv', latent_out.astype(jnp.float32), wv_up.astype(jnp.float32)).astype(jnp.bfloat16).reshape(total, H * VD)
    hidden = residual.astype(jnp.float32) + jnp.dot(heads_out, w_out, preferred_element_type=jnp.float32)
    normed = normalize(hidden, ffn_gain)

    def dispatch(group_args):
        ids_group, normed_group = group_args
        names = lax.optimization_barrier(jnp.sum((ids_group[:, :, None] == jnp.arange(EXPERTS, dtype=jnp.int32)[None, None, :]).astype(jnp.int32), 1))
        before = jnp.cumsum(names, 0) - names
        slot_ids = jnp.arange(CAP, dtype=jnp.int32)
        pick = ((names.T[:, None, :] == 1) & (before.T[:, None, :] == slot_ids[None, :, None])).astype(jnp.float32)
        return jnp.einsum('xso,od->xsd', pick, normed_group.astype(jnp.float32)).astype(jnp.bfloat16)
    expert_in = lax.map(dispatch, (expert_ids.reshape(N_CTX, ROWS, TOPK), normed.reshape(N_CTX, ROWS, D)))
    return (hidden.astype(jnp.bfloat16), expert_in)
```

```python
import math

import jax
import jax.numpy as jnp
import numpy as np
from jax import lax
from jax.experimental import pallas as pl
from jax.experimental.pallas import tpu as pltpu
from jax.sharding import PartitionSpec as P

MESH = pl.DeviceIdType.MESH
F32 = jnp.float32
BF16 = jnp.bfloat16
N_CTX, N_EXP, N_X, N_Z = 8, 64, 4, 16
ROWS, LLOC, LAT, KVL, NOPE, RD, VD = 64, 8, 576, 512, 128, 64, 128
QL, D, CAP = 1536, 7168, 4
QW = NOPE + RD
COLS = D // 8
LANES = D // 128
SCALE = 1.0 / math.sqrt(QW)


def dot(a, b, ca=1, cb=0):
    return lax.dot_general(a, b, (((ca,), (cb,)), ((), ())), preferred_element_type=F32)


def send(src, dst, send_sem, recv_sem, device):
    pltpu.make_async_remote_copy(
        src_ref=src,
        dst_ref=dst,
        send_sem=send_sem,
        recv_sem=recv_sem,
        device_id=device,
        device_id_type=MESH,
    ).start()


def drain(ref, sem):
    pltpu.make_async_copy(ref, ref, sem).wait()


def each(low, high, body):
    def step(k, carry):
        body(k)
        return carry

    lax.fori_loop(low, high, step, 0)


def kernel(
    owner_s,
    lens_s,
    owner_g,
    owner_row,
    lens_g,
    freqs,
    ids,
    residual,
    gain,
    cache_hbm,
    ql_hbm,
    nl_hbm,
    wq_hbm,
    wk_hbm,
    wv_hbm,
    wo_hbm,
    hidden_ref,
    expert_ref,
    ql,
    wq,
    wk,
    wv,
    kbuf,
    qall,
    nlall,
    qsend,
    qrecv,
    lsend,
    lrecv,
    hall,
    wbuf,
    psend,
    precv,
    rsend,
    rrecv,
    flat,
    nbuf,
    idx_v,
    idx_s,
    load_sem,
    own_sem,
    send_sem,
    recv_sem,
    z_sem,
):
    c = lax.axis_index("ctx")
    e = lax.axis_index("exp")
    y, core = c // 2, lax.rem(c, 2)
    z, x = e // N_X, lax.rem(e, N_X)

    loads = [
        pltpu.make_async_copy(src, dst, load_sem.at[i])
        for i, (src, dst) in enumerate(
            [
                (ql_hbm, ql),
                (wq_hbm, wq),
                (wk_hbm, wk),
                (wv_hbm, wv),
                (nl_hbm, nlall.at[c]),
            ]
        )
    ]
    for load in loads:
        load.start()

    barrier = pltpu.get_barrier_semaphore()

    def greet(device):
        pl.semaphore_signal(barrier, inc=1, device_id=device, device_id_type=MESH)

    each(1, N_EXP, lambda k: greet((c, lax.rem(e + k, N_EXP))))

    def greet_plane(k):
        for i in range(N_X):
            greet((lax.rem(c + k, N_CTX), z * N_X + i))

    each(1, N_CTX, greet_plane)

    loads[0].wait()
    loads[1].wait()
    qall[c] = dot(ql[...], wq[...], 1, 1).astype(BF16)
    loads[4].wait()

    pl.semaphore_wait(barrier, N_EXP - 1 + (N_CTX - 1) * N_X)

    def send_q(k):
        to = (lax.rem(c + k, N_CTX), e)
        send(qall.at[c], qall.at[c], send_sem.at[0], recv_sem.at[0], to)

    each(1, N_CTX, send_q)

    own = pltpu.make_async_copy(cache_hbm.at[e], kbuf.at[e], recv_sem.at[1])
    own.start()

    def send_cache(k):
        j = lax.rem(e + k, N_EXP)
        send(cache_hbm.at[j], kbuf.at[e], send_sem.at[1], recv_sem.at[1], (c, j))

    each(1, N_EXP, send_cache)

    def send_new(k):
        to = (lax.rem(c + k, N_CTX), e)
        send(nlall.at[c], nlall.at[c], send_sem.at[2], recv_sem.at[2], to)

    each(1, N_CTX, send_new)

    def columns(i):
        return wo_hbm.at[:, pl.ds(pl.multiple_of((i * 2 + core) * COLS, 128), COLS)]

    own_w = pltpu.make_async_copy(columns(x), wbuf.at[x], own_sem)
    own_w.start()

    def send_w(k):
        i = lax.rem(x + k, N_X)
        send(columns(i), wbuf.at[x], send_sem.at[3], recv_sem.at[3], (c, z * N_X + i))

    each(1, N_X, send_w)

    names = ids[...]
    row = lax.broadcasted_iota(jnp.int32, (8, ROWS), 0)
    named = jnp.zeros((8, ROWS), F32)
    for i in range(4):
        hit = jnp.sum((names == e * 4 + i).astype(F32), 0, keepdims=True)
        named = jnp.where(row == i, hit, named)
    earlier = (
        lax.broadcasted_iota(jnp.int32, (ROWS, ROWS), 0)
        < lax.broadcasted_iota(jnp.int32, (ROWS, ROWS), 1)
    ).astype(F32)
    before = dot(named.astype(BF16), earlier.astype(BF16))
    number = lax.broadcasted_iota(jnp.int32, (8, ROWS), 1).astype(F32) + 1.0
    lane = lax.broadcasted_iota(jnp.int32, (8, 128), 1)
    chosen = jnp.zeros((8, 128), F32)
    for s in range(CAP):
        taken = jnp.where((before == s) & (named > 0.5), number, 0.0)
        chosen = jnp.where(lane == s, jnp.sum(taken, 1, keepdims=True), chosen)
    idx_v[...] = chosen.astype(jnp.int32)
    to_scalar = pltpu.make_async_copy(idx_v, idx_s, load_sem.at[5])
    to_scalar.start()

    mine = owner_g[pl.ds(c, 1), :]
    place = (lax.broadcasted_iota(jnp.int32, (N_CTX * ROWS, ROWS), 0) == mine).astype(F32)
    lengths = lens_g[pl.ds(c, 1), :].astype(F32)
    eye = lax.broadcasted_iota(jnp.int32, (ROWS, ROWS), 0) == lax.broadcasted_iota(
        jnp.int32, (ROWS, ROWS), 1
    )
    angles = jnp.sum(jnp.where(eye, lengths, 0.0), 1, keepdims=True) * freqs[...]
    cosines, sines = jnp.cos(angles), jnp.sin(angles)
    loads[2].wait()
    drain(qall.at[pl.ds(0, N_CTX - 1)], recv_sem.at[0])
    q = dot(place.astype(BF16), qall[...].reshape(N_CTX * ROWS, QW), 0, 0)
    absorbed = dot(q[:, :NOPE].astype(BF16), wk[...])
    first, second = q[:, NOPE : NOPE + RD // 2], q[:, NOPE + RD // 2 :]
    turned = jnp.concatenate(
        [first * cosines - second * sines, first * sines + second * cosines], 1
    )
    qsend[:, 0, :KVL] = absorbed.astype(BF16).astype(F32)
    qsend[:, 0, KVL:] = turned.astype(BF16).astype(F32)
    qrecv[e] = qsend[e]

    def send_query(k):
        j = lax.rem(e + k, N_EXP)
        send(qsend.at[j], qrecv.at[e], send_sem.at[4], recv_sem.at[4], (c, j))

    each(1, N_EXP, send_query)

    request = c * ROWS + e
    length = lens_s[request]
    slot = owner_s[request]
    drain(nlall.at[pl.ds(0, N_CTX - 1)], recv_sem.at[2])
    pick = (lax.broadcasted_iota(jnp.int32, (16, N_CTX * ROWS), 1) == slot).astype(F32)
    new = dot(pick.astype(BF16), nlall[...].reshape(N_CTX * ROWS, LAT))[0:1, :]
    drain(qrecv.at[pl.ds(0, N_EXP - 1)], recv_sem.at[4])
    queries = qrecv[:, 0, :]
    new_scores = jnp.sum(queries * new, 1, keepdims=True) * SCALE
    queries = queries.astype(BF16)
    drain(kbuf, recv_sem.at[1])
    keys = kbuf[...].astype(F32).reshape(N_EXP * LLOC, LAT).astype(BF16)
    scores = dot(queries, keys, 1, 1) * SCALE
    valid = lax.broadcasted_iota(jnp.int32, scores.shape, 1) < length
    top = jnp.max(jnp.where(valid, scores, -1e30), 1, keepdims=True)
    top = jnp.maximum(top, new_scores)
    weights = jnp.where(valid, jnp.exp(scores - top), 0.0)
    new_weight = jnp.exp(new_scores - top)
    total = jnp.sum(weights, 1, keepdims=True) + new_weight
    mixed = dot(weights.astype(BF16), keys[:, :KVL])
    mixed = mixed + new_weight.astype(BF16).astype(F32) * new[:, :KVL]
    lsend[:, 0, :] = (mixed / total).astype(BF16).astype(F32)
    lrecv[e] = lsend[e]

    def send_latent(k):
        j = lax.rem(e + k, N_EXP)
        send(lsend.at[j], lrecv.at[e], send_sem.at[5], recv_sem.at[5], (c, j))

    each(1, N_EXP, send_latent)

    loads[3].wait()
    drain(lrecv.at[pl.ds(0, N_EXP - 1)], recv_sem.at[5])
    at = c * N_X + x
    hall[at] = dot(lrecv[:, 0, :].astype(BF16), wv[...]).astype(BF16)

    def send_heads(k):
        to_c = lax.rem(c + k, N_CTX)
        for i in range(N_X):
            to_x = lax.rem(x + i, N_X)
            send(hall.at[at], hall.at[at], send_sem.at[6], recv_sem.at[6], (to_c, z * N_X + to_x))

    def send_heads_x(k):
        to_x = lax.rem(x + k, N_X)
        send(hall.at[at], hall.at[at], send_sem.at[6], recv_sem.at[6], (c, z * N_X + to_x))

    each(1, N_CTX, send_heads)
    each(1, N_X, send_heads_x)

    order = lax.broadcasted_iota(jnp.int32, (2 * ROWS, N_CTX * ROWS), 0)
    rest = order % 8
    wanted = (y * 2 + rest // N_X) * ROWS + (order // 8) * N_X + rest % N_X
    place = (owner_row[...] == wanted).astype(F32).astype(BF16)
    own_w.wait()
    drain(wbuf.at[pl.ds(0, N_X - 1)], recv_sem.at[3])
    drain(hall.at[pl.ds(0, N_CTX * N_X - 1)], recv_sem.at[6])
    partial = jnp.zeros((2 * ROWS, COLS), F32)
    heads = hall[...].reshape(N_CTX, N_X, ROWS, VD)
    for i in range(N_X):
        head = dot(place, heads[:, i].reshape(N_CTX * ROWS, VD)).astype(BF16)
        partial = partial + dot(head, wbuf[i])
    psend[...] = partial.reshape(N_Z, 8, COLS)
    precv[z] = psend[z]

    def send_partial(k):
        to_z = lax.rem(z + k, N_Z)
        send(psend.at[to_z], precv.at[z], send_sem.at[7], recv_sem.at[7], (c, to_z * N_X + x))

    each(1, N_Z, send_partial)
    drain(precv.at[pl.ds(0, N_Z - 1)], recv_sem.at[7])
    summed = precv[0]
    for i in range(1, N_Z):
        summed = summed + precv[i]

    rsend[:, 0, :] = summed
    mine_row, block = core * N_X + x, x * 2 + core
    rrecv[block] = rsend[mine_row]

    def send_row(k):
        j = lax.rem(mine_row + k, 8)
        to = (y * 2 + j // N_X, z * N_X + lax.rem(j, N_X))
        send(rsend.at[j], rrecv.at[block], send_sem.at[8], recv_sem.at[8], to)

    each(1, 8, send_row)
    drain(rrecv.at[pl.ds(0, 7)], recv_sem.at[8])
    hidden = residual[...].astype(F32) + rrecv[:, 0, :]
    hidden_ref[...] = hidden.astype(BF16)
    square = jnp.sum(jnp.sum(hidden * hidden, 1, keepdims=True), 0, keepdims=True)
    normed = hidden * lax.rsqrt(square * (1.0 / D) + 1e-06) * gain[...]
    for i in range(COLS // 128):
        flat[pl.ds(i, 8, stride=COLS // 128), :] = normed[:, i * 128 : (i + 1) * 128]
    nbuf[e] = flat[0:LANES, :].astype(BF16)

    def send_z(k):
        to_z = lax.rem(z + k, N_Z)
        send(nbuf.at[e], nbuf.at[e], send_sem.at[9], z_sem.at[z], (c, to_z * N_X + x))

    each(1, N_Z, send_z)

    def forward(k):
        from_z = lax.rem(z + N_Z - k, N_Z)
        at_row = from_z * N_X + x

        @pl.when(k > 0)
        def _():
            drain(nbuf.at[at_row], z_sem.at[from_z])

        for i in range(1, N_X):
            to_x = lax.rem(x + i, N_X)
            send(
                nbuf.at[at_row], nbuf.at[at_row], send_sem.at[10], recv_sem.at[9], (c, z * N_X + to_x)
            )

    each(0, N_Z, forward)
    to_scalar.wait()
    drain(nbuf.at[pl.ds(0, N_Z * (N_X - 1))], recv_sem.at[9])
    for i in range(4):
        for s in range(CAP):
            found = idx_s[i, s]
            rows = nbuf[jnp.clip(found - 1, 0, N_EXP - 1)].astype(F32)
            expert_ref[i * CAP + s] = jnp.where(found > 0, rows, 0.0).astype(BF16)

    drain(qall.at[pl.ds(0, N_CTX - 1)], send_sem.at[0])
    drain(kbuf.at[pl.ds(0, N_EXP - 1)], send_sem.at[1])
    drain(nlall.at[pl.ds(0, N_CTX - 1)], send_sem.at[2])
    drain(wbuf.at[pl.ds(0, N_X - 1)], send_sem.at[3])
    drain(qsend.at[pl.ds(0, N_EXP - 1)], send_sem.at[4])
    drain(lsend.at[pl.ds(0, N_EXP - 1)], send_sem.at[5])
    drain(hall.at[pl.ds(0, N_CTX * N_X - 1)], send_sem.at[6])
    drain(psend.at[pl.ds(0, N_Z - 1)], send_sem.at[7])
    drain(rsend.at[pl.ds(0, 7)], send_sem.at[8])
    drain(nbuf.at[pl.ds(0, N_Z - 1)], send_sem.at[9])
    drain(nbuf.at[pl.ds(0, N_Z * (N_X - 1))], send_sem.at[10])


def on_device(
    prefill_cache,
    owner_slot,
    cached_len,
    query_latent,
    new_latent,
    wq_up,
    wk_up,
    wv_up,
    w_out,
    residual,
    ffn_gain,
    expert_ids,
):
    half = (10000.0 ** (-2.0 * np.arange(RD // 2, dtype=np.float32) / RD)).astype(np.float32)
    smem = pl.BlockSpec(memory_space=pltpu.SMEM)
    vmem = pl.BlockSpec(memory_space=pltpu.VMEM)
    anywhere = pl.BlockSpec(memory_space=pl.ANY)
    hidden, expert_in = pl.pallas_call(
        kernel,
        out_shape=(
            jax.ShapeDtypeStruct((8, COLS), BF16),
            jax.ShapeDtypeStruct((4 * CAP, LANES, 128), BF16),
        ),
        in_specs=[smem] * 2 + [vmem] * 7 + [anywhere] * 7,
        out_specs=(vmem, vmem),
        scratch_shapes=[
            pltpu.VMEM((ROWS, QL), BF16),
            pltpu.VMEM((QW, QL), BF16),
            pltpu.VMEM((NOPE, KVL), BF16),
            pltpu.VMEM((KVL, VD), BF16),
            pltpu.VMEM((N_EXP, LLOC, LAT), BF16),
            pltpu.VMEM((N_CTX, ROWS, QW), BF16),
            pltpu.VMEM((N_CTX, ROWS, LAT), BF16),
            pltpu.VMEM((ROWS, 1, LAT), F32),
            pltpu.VMEM((N_EXP, 1, LAT), F32),
            pltpu.VMEM((N_EXP, 1, KVL), F32),
            pltpu.VMEM((ROWS, 1, KVL), F32),
            pltpu.VMEM((N_CTX * N_X, ROWS, VD), BF16),
            pltpu.VMEM((N_X, VD, COLS), BF16),
            pltpu.VMEM((N_Z, 8, COLS), F32),
            pltpu.VMEM((N_Z, 8, COLS), F32),
            pltpu.VMEM((8, 1, COLS), F32),
            pltpu.VMEM((8, 1, COLS), F32),
            pltpu.VMEM((64, 128), F32),
            pltpu.VMEM((N_EXP, LANES, 128), BF16),
            pltpu.VMEM((8, 128), jnp.int32),
            pltpu.SMEM((8, 128), jnp.int32),
            pltpu.SemaphoreType.DMA((6,)),
            pltpu.SemaphoreType.DMA,
            pltpu.SemaphoreType.DMA((11,)),
            pltpu.SemaphoreType.DMA((10,)),
            pltpu.SemaphoreType.DMA((N_Z,)),
        ],
        compiler_params=pltpu.CompilerParams(
            collective_id=0, has_side_effects=True, vmem_limit_bytes=60 * 1024 * 1024
        ),
        cost_estimate=pl.CostEstimate(
            flops=600_000_000, bytes_accessed=8_000_000, transcendentals=40_000
        ),
    )(
        owner_slot,
        cached_len,
        owner_slot.reshape(N_CTX, ROWS),
        owner_slot.reshape(1, N_CTX * ROWS),
        cached_len.reshape(N_CTX, ROWS),
        jnp.asarray(half).reshape(1, RD // 2),
        expert_ids.T,
        residual.reshape(8, COLS),
        ffn_gain.reshape(8, COLS),
        prefill_cache,
        query_latent,
        new_latent,
        wq_up.reshape(QL, QW).T,
        wk_up.reshape(NOPE, KVL),
        wv_up.reshape(KVL, VD),
        w_out,
    )
    return hidden.reshape(1, D), expert_in.reshape(1, 4, CAP, D)


def solution(mesh):
    placed = (
        P("ctx", "exp", None),
        P(),
        P(),
        P("ctx", None),
        P("ctx", None),
        P(None, "exp", None),
        P("exp", None, None),
        P("exp", None, None),
        P("exp", None),
        P(("ctx", "exp"), None),
        P(),
        P("ctx", None),
    )
    return jax.shard_map(
        on_device,
        mesh=mesh,
        in_specs=placed,
        out_specs=(P(("ctx", "exp"), None), P("ctx", "exp", None, None)),
        check_vma=False,
    )
```

```python
import math

import jax
import jax.numpy as jnp
import numpy as np
from jax import lax
from jax.experimental import pallas as pl
from jax.experimental.pallas import tpu as pltpu
from jax.sharding import PartitionSpec as P

MESH = pl.DeviceIdType.MESH
F32 = jnp.float32
BF16 = jnp.bfloat16
N_CTX, N_EXP, N_X, N_Z = 8, 64, 4, 16
ROWS, LLOC, LAT, KVL, NOPE, RD, VD = 64, 8, 576, 512, 128, 64, 128
QL, D, CAP = 1536, 7168, 4
QW = NOPE + RD
COLS = D // 8
PAIRS, NEAR = ROWS // 2, N_Z // 2
SCALE = 1.0 / math.sqrt(QW)


def dot(a, b, ca=1, cb=0):
    return lax.dot_general(a, b, (((ca,), (cb,)), ((), ())), preferred_element_type=F32)


def send(src, dst, send_sem, recv_sem, device):
    pltpu.make_async_remote_copy(
        src_ref=src,
        dst_ref=dst,
        send_sem=send_sem,
        recv_sem=recv_sem,
        device_id=device,
        device_id_type=MESH,
    ).start()


def drain(ref, sem):
    pltpu.make_async_copy(ref, ref, sem).wait()


def each(low, high, body):
    def step(k, carry):
        body(k)
        return carry

    lax.fori_loop(low, high, step, 0)


def offset(i, size):
    far = size // 2 - i // 2
    return jnp.where(i % 2 == 0, far, size - far)


def split(value):
    high = value.astype(BF16).astype(F32)
    middle = (value - high).astype(BF16).astype(F32)
    return high, middle, value - high - middle


def own_part(row, y, core):
    part = row[:, 0:128]
    for i in range(1, N_CTX // 2):
        part = jnp.where(y == i, row[:, i * 128 : (i + 1) * 128], part)
    return jnp.where(core == 0, part[:, :ROWS], part[:, ROWS:])


def kernel(
    owner_s,
    lens_s,
    owner_row,
    lens_row,
    freqs,
    ids,
    residual,
    gain,
    cache_hbm,
    ql_hbm,
    nl_hbm,
    wq_hbm,
    wk_hbm,
    wv_hbm,
    wo_hbm,
    hidden_ref,
    expert_ref,
    ql,
    wq,
    wk,
    wv,
    kbuf,
    qall,
    nlall,
    qsend,
    qrecv,
    lsend,
    lrecv,
    hall,
    wbuf,
    psend,
    precv,
    rsend,
    resid,
    zbuf,
    gbuf,
    load_sem,
    own_sem,
    send_sem,
    recv_sem,
    z_sem,
):
    c = lax.axis_index("ctx")
    e = lax.axis_index("exp")
    y, core = c // 2, lax.rem(c, 2)
    z, x = e // N_X, lax.rem(e, N_X)

    loads = [
        pltpu.make_async_copy(src, dst, load_sem.at[i])
        for i, (src, dst) in enumerate(
            [
                (ql_hbm, ql),
                (wq_hbm, wq),
                (wk_hbm, wk),
                (wv_hbm, wv),
                (nl_hbm, nlall.at[c]),
            ]
        )
    ]
    for load in loads:
        load.start()

    barrier = pltpu.get_barrier_semaphore()
    sent, due = [], {}

    def track(name, ref, i):
        sent.append((ref, send_sem.at[i]))
        due[name] = (ref, recv_sem.at[i])

    def arrive(name):
        drain(*due.pop(name))

    def greet(device):
        pl.semaphore_signal(barrier, inc=1, device_id=device, device_id_type=MESH)

    each(1, N_EXP, lambda k: greet((c, lax.rem(e + k, N_EXP))))

    def greet_plane(k):
        for i in range(N_X):
            greet((lax.rem(c + k, N_CTX), z * N_X + i))

    each(1, N_CTX, greet_plane)

    loads[0].wait()
    loads[1].wait()
    qall[c] = dot(ql[...], wq[...], 1, 1).astype(BF16)
    loads[4].wait()

    pl.semaphore_wait(barrier, N_EXP - 1 + (N_CTX - 1) * N_X)

    def send_q(k):
        to = (lax.rem(c + offset(k, N_CTX), N_CTX), e)
        send(qall.at[c], qall.at[c], send_sem.at[0], recv_sem.at[0], to)

    each(1, N_CTX, send_q)
    track("q", qall.at[pl.ds(0, N_CTX - 1)], 0)

    pair = lax.rem(e, PAIRS)
    own = pltpu.make_async_copy(
        cache_hbm.at[pl.ds(2 * pair, 2)], kbuf.at[NEAR // 2 * N_X + x], recv_sem.at[1]
    )
    own.start()

    def send_cache(i):
        step = i // N_X
        near = NEAR // 2 - (step + 1) // 2
        away = jnp.where(step % 2 == 1, near, N_Z - near)
        away = jnp.where((step == 0) & (z % 2 == 0), NEAR // 2, away)
        to_z = lax.rem(z + away, N_Z)
        to_x = lax.rem(x + i + jnp.where(step == NEAR - 1, 1, 0), N_X)
        into = lax.rem(N_Z - away + NEAR // 2, NEAR) * N_X + x
        pairs = pl.ds(2 * (lax.rem(to_z, NEAR) * N_X + to_x), 2)
        send(cache_hbm.at[pairs], kbuf.at[into], send_sem.at[1], recv_sem.at[1], (c, to_z * N_X + to_x))

    each(0, PAIRS - 1, send_cache)
    sent.append((kbuf.at[pl.ds(0, PAIRS - 1)], send_sem.at[1]))
    due["cache"] = (kbuf, recv_sem.at[1])

    def send_new(k):
        to = (lax.rem(c + offset(k, N_CTX), N_CTX), e)
        send(nlall.at[c], nlall.at[c], send_sem.at[2], recv_sem.at[2], to)

    each(1, N_CTX, send_new)
    track("new", nlall.at[pl.ds(0, N_CTX - 1)], 2)

    mine_row, block = core * N_X + x, x * 2 + core
    for i in range(8):
        rsend[i] = residual[:, i * COLS : (i + 1) * COLS].astype(F32)
    resid[mine_row] = rsend[block]

    def send_residual(k):
        to_x, to_core = lax.rem(x + k // 2, N_X), lax.rem(core + k, 2)
        to = (y * 2 + to_core, z * N_X + to_x)
        send(rsend.at[to_x * 2 + to_core], resid.at[mine_row], send_sem.at[8], recv_sem.at[8], to)

    each(1, 8, send_residual)
    track("residual", resid.at[pl.ds(0, 7)], 8)

    names = ids[...]
    row = lax.broadcasted_iota(jnp.int32, (8, ROWS), 0)
    named = jnp.zeros((8, ROWS), F32)
    for i in range(4):
        hit = jnp.sum((names == e * 4 + i).astype(F32), 0, keepdims=True)
        named = jnp.where(row == i, hit, named)
    earlier = (
        lax.broadcasted_iota(jnp.int32, (ROWS, ROWS), 0)
        < lax.broadcasted_iota(jnp.int32, (ROWS, ROWS), 1)
    ).astype(F32)
    before = dot(named.astype(BF16), earlier.astype(BF16))
    column = lax.broadcasted_iota(jnp.int32, (24, ROWS), 1)
    line = lax.broadcasted_iota(jnp.int32, (24, ROWS), 0)
    selection = jnp.where((line == 4 * CAP) & (column == e), 1.0, 0.0)
    for i in range(4):
        for s in range(CAP):
            taken = jnp.where((before[i : i + 1] == s) & (named[i : i + 1] > 0.5), 1.0, 0.0)
            selection = jnp.where(line == i * CAP + s, taken, selection)
    stage = lax.broadcasted_iota(jnp.int32, (1, ROWS), 1) // N_X
    stage = jnp.where(stage == 0, z, z + N_Z - offset(stage, N_Z)) % N_Z
    held = stage * N_X + lax.broadcasted_iota(jnp.int32, (1, ROWS), 1) % N_X
    held = (lax.broadcasted_iota(jnp.int32, (ROWS, ROWS), 0) == held).astype(F32)
    selection = dot(selection.astype(BF16), held.astype(BF16)).astype(BF16)

    mine = own_part(owner_row[...], y, core)
    place = (lax.broadcasted_iota(jnp.int32, (N_CTX * ROWS, ROWS), 0) == mine).astype(F32)
    lengths = own_part(lens_row[...], y, core).astype(F32)
    eye = lax.broadcasted_iota(jnp.int32, (ROWS, ROWS), 0) == lax.broadcasted_iota(
        jnp.int32, (ROWS, ROWS), 1
    )
    angles = jnp.sum(jnp.where(eye, lengths, 0.0), 1, keepdims=True) * freqs[...]
    cosines, sines = jnp.cos(angles), jnp.sin(angles)
    loads[2].wait()
    arrive("q")
    q = dot(place.astype(BF16), qall[...].reshape(N_CTX * ROWS, QW), 0, 0)
    absorbed = dot(q[:, :NOPE].astype(BF16), wk[...])
    first, second = q[:, NOPE : NOPE + RD // 2], q[:, NOPE + RD // 2 :]
    turned = jnp.concatenate(
        [first * cosines - second * sines, first * sines + second * cosines], 1
    )
    absorbed = jnp.concatenate([absorbed, turned], 1).astype(BF16)
    qsend[...] = absorbed.reshape(PAIRS, 2, LAT)
    own_query = pltpu.make_async_copy(qsend.at[pair], qrecv.at[e], own_sem.at[1])
    own_query.start()
    due["own_query"] = (qrecv.at[e], own_sem.at[1])

    def send_query(k):
        j = lax.rem(e + offset(k, N_EXP), N_EXP)
        send(qsend.at[lax.rem(j, PAIRS)], qrecv.at[e], send_sem.at[4], recv_sem.at[4], (c, j))

    each(1, N_EXP, send_query)
    track("query", qrecv.at[pl.ds(0, N_EXP - 1)], 4)

    def columns(i):
        return wo_hbm.at[:, pl.ds(pl.multiple_of((i * 2 + core) * COLS, 128), COLS)]

    own_w = pltpu.make_async_copy(columns(x), wbuf.at[x], own_sem.at[0])
    own_w.start()
    due["own_w"] = (wbuf.at[x], own_sem.at[0])

    def send_w(k):
        i = lax.rem(x + k, N_X)
        send(columns(i), wbuf.at[x], send_sem.at[3], recv_sem.at[3], (c, z * N_X + i))

    each(1, N_X, send_w)
    track("w", wbuf.at[pl.ds(0, N_X - 1)], 3)

    first_request = c * ROWS + 2 * pair
    width = PAIRS * LLOC
    slot = lax.broadcasted_iota(jnp.int32, (1, width), 1) // LLOC
    from_z = z + slot // N_X + N_Z - NEAR // 2
    from_z = jnp.where((slot < N_X) & (z % 2 == 1), z + NEAR // 2, from_z) % N_Z
    position = (from_z * N_X + slot % N_X) * LLOC
    position = position + lax.broadcasted_iota(jnp.int32, (1, width), 1) % LLOC
    even = lax.broadcasted_iota(jnp.int32, (2 * N_EXP, 1), 0) % 2 == 0
    valid = position < jnp.where(even, lens_s[first_request], lens_s[first_request + 1])
    chosen = lax.broadcasted_iota(jnp.int32, (16, 1), 0)
    chosen = jnp.where(chosen == 0, owner_s[first_request], owner_s[first_request + 1])
    pick = (lax.broadcasted_iota(jnp.int32, (16, N_CTX * ROWS), 1) == chosen).astype(F32)
    arrive("new")
    new = dot(pick.astype(BF16), nlall[...].reshape(N_CTX * ROWS, LAT))
    arrive("own_query")
    arrive("query")
    queries = qrecv[...].reshape(2 * N_EXP, LAT)
    new_scores = dot(queries, new.astype(BF16), 1, 1) * SCALE
    new_scores = jnp.where(even, new_scores[:, 0:1], new_scores[:, 1:2])
    new_scores = jnp.where(e < PAIRS, new_scores, -1e30)
    arrive("cache")
    keys = [kbuf[:, t].astype(F32).reshape(width, LAT).astype(BF16) for t in range(2)]
    scores = jnp.where(even, dot(queries, keys[0], 1, 1), dot(queries, keys[1], 1, 1)) * SCALE
    top = jnp.max(jnp.where(valid, scores, -1e30), 1, keepdims=True)
    top = jnp.maximum(top, new_scores)
    weights = jnp.where(valid, jnp.exp(scores - top), 0.0)
    new_weight = jnp.where(e < PAIRS, jnp.exp(new_scores - top), 0.0)
    total = jnp.sum(weights, 1, keepdims=True) + new_weight
    mixed = dot(jnp.where(even, weights, 0.0).astype(BF16), keys[0][:, :KVL])
    mixed = mixed + dot(jnp.where(even, 0.0, weights).astype(BF16), keys[1][:, :KVL])
    mixed = mixed + new_weight.astype(BF16).astype(F32) * jnp.where(
        even, new[0:1, :KVL], new[1:2, :KVL]
    )
    some = total > 0.0
    divisor = jnp.where(some, total, 1.0)
    parts = split(jnp.where(some, top + jnp.log(divisor), -1e30))
    lane = lax.broadcasted_iota(jnp.int32, (2 * N_EXP, 128), 1)
    tail = jnp.zeros((2 * N_EXP, 128), F32)
    for i in range(3):
        tail = jnp.where(lane == i, parts[i], tail)
    latent = jnp.concatenate([mixed / divisor, tail], 1).astype(BF16)
    lsend[...] = latent.reshape(N_EXP, 2, KVL + 128)
    own_latent = pltpu.make_async_copy(lsend.at[e], lrecv.at[e], own_sem.at[2])
    own_latent.start()
    due["own_latent"] = (lrecv.at[e], own_sem.at[2])

    def send_latent(k):
        j = lax.rem(e + offset(k, N_EXP), N_EXP)
        send(lsend.at[j], lrecv.at[e], send_sem.at[5], recv_sem.at[5], (c, j))

    each(1, N_EXP, send_latent)
    track("latent", lrecv.at[pl.ds(0, N_EXP - 1)], 5)

    loads[3].wait()
    arrive("own_latent")
    arrive("latent")
    at = c * N_X + x
    halves = lrecv[...].reshape(2 * N_EXP, KVL + 128).astype(F32)
    sums = halves[:, KVL : KVL + 1] + halves[:, KVL + 1 : KVL + 2] + halves[:, KVL + 2 : KVL + 3]
    peak = jnp.maximum(sums[:ROWS], sums[ROWS:])
    low, high = jnp.exp(sums[:ROWS] - peak), jnp.exp(sums[ROWS:] - peak)
    latent = (low * halves[:ROWS, :KVL] + high * halves[ROWS:, :KVL]) / (low + high)
    hall[at] = dot(latent.astype(BF16), wv[...]).astype(BF16)

    def send_heads(k):
        to_c = lax.rem(c + offset(k, N_CTX), N_CTX)
        for i in range(N_X):
            to_x = lax.rem(x + i, N_X)
            send(hall.at[at], hall.at[at], send_sem.at[6], recv_sem.at[6], (to_c, z * N_X + to_x))

    def send_heads_x(k):
        to_x = lax.rem(x + k, N_X)
        send(hall.at[at], hall.at[at], send_sem.at[6], recv_sem.at[6], (c, z * N_X + to_x))

    each(1, N_CTX, send_heads)
    each(1, N_X, send_heads_x)
    track("heads", hall.at[pl.ds(0, N_CTX * N_X - 1)], 6)

    order = lax.broadcasted_iota(jnp.int32, (2 * ROWS, N_CTX * ROWS), 0)
    rest = order % 8
    wanted = (y * 2 + rest // N_X) * ROWS + (order // 8) * N_X + rest % N_X
    place = (owner_row[...] == wanted).astype(F32).astype(BF16)
    arrive("own_w")
    arrive("w")
    arrive("heads")
    partial = jnp.zeros((2 * ROWS, COLS), F32)
    heads = hall[...].reshape(N_CTX, N_X, ROWS, VD)
    for i in range(N_X):
        head = dot(place, heads[:, i].reshape(N_CTX * ROWS, VD)).astype(BF16)
        partial = partial + dot(head, wbuf[i])
    psend[...] = partial.reshape(N_Z, 8, COLS).astype(BF16)
    precv[z] = psend[z]

    def send_partial(k):
        to_z = lax.rem(z + offset(k, N_Z), N_Z)
        send(psend.at[to_z], precv.at[z], send_sem.at[7], recv_sem.at[7], (c, to_z * N_X + x))

    each(1, N_Z, send_partial)
    track("partial", precv.at[pl.ds(0, N_Z - 1)], 7)
    arrive("partial")
    summed = precv[0].astype(F32)
    for i in range(1, N_Z):
        summed = summed + precv[i].astype(F32)

    arrive("residual")
    hidden = (summed + resid[:, 0, :]).astype(BF16)
    zbuf[0] = hidden.reshape(2, N_X, COLS)

    def send_z(k):
        to_z = lax.rem(z + offset(k, N_Z), N_Z)
        send(zbuf.at[0], zbuf.at[k], send_sem.at[9], z_sem.at[k], (c, to_z * N_X + x))

    def spread(low, size):
        here = pl.ds(low, size)
        for k in range(1, 8):
            to_x, to_core = lax.rem(x + k // 2, N_X), lax.rem(core + k, 2)
            to = (y * 2 + to_core, z * N_X + to_x)
            send(zbuf.at[here, to_core], gbuf.at[block, here], send_sem.at[10], recv_sem.at[10], to)

    def landed(k):
        drain(zbuf.at[k], z_sem.at[k])

    each(1, 8, send_z)
    spread(0, 1)
    each(1, 4, landed)
    each(8, 12, send_z)
    spread(1, 3)
    each(4, 8, landed)
    each(12, 16, send_z)
    spread(4, 4)
    each(8, 12, landed)
    spread(8, 4)
    each(12, 16, landed)
    spread(12, 4)
    sent.append((zbuf.at[pl.ds(0, N_Z - 1)], send_sem.at[9]))
    track("rows", gbuf.at[pl.ds(0, 7)], 10)
    gbuf[block] = zbuf[:, core]
    arrive("rows")

    picked = []
    square = jnp.zeros((24, 1), F32)
    for i in range(8):
        rows = dot(selection, gbuf[i].reshape(ROWS, COLS))
        square = square + jnp.sum(rows * rows, 1, keepdims=True)
        picked.append(rows)
    factor = lax.rsqrt(square * (1.0 / D) + 1e-06)
    for i in range(8):
        there = slice(i * COLS, (i + 1) * COLS)
        hidden_ref[:, there] = picked[i][4 * CAP : 4 * CAP + 1].astype(BF16)
        expert_ref[:, there] = (picked[i] * factor * gain[:, there])[: 4 * CAP].astype(BF16)

    for ref, sem in sent:
        drain(ref, sem)


def on_device(
    prefill_cache,
    owner_slot,
    cached_len,
    query_latent,
    new_latent,
    wq_up,
    wk_up,
    wv_up,
    w_out,
    residual,
    ffn_gain,
    expert_ids,
):
    half = (10000.0 ** (-2.0 * np.arange(RD // 2, dtype=np.float32) / RD)).astype(np.float32)
    smem = pl.BlockSpec(memory_space=pltpu.SMEM)
    vmem = pl.BlockSpec(memory_space=pltpu.VMEM)
    anywhere = pl.BlockSpec(memory_space=pl.ANY)
    hidden, expert_in = pl.pallas_call(
        kernel,
        out_shape=(
            jax.ShapeDtypeStruct((1, D), BF16),
            jax.ShapeDtypeStruct((4 * CAP, D), BF16),
        ),
        in_specs=[smem] * 2 + [vmem] * 6 + [anywhere] * 7,
        out_specs=(vmem, vmem),
        scratch_shapes=[
            pltpu.VMEM((ROWS, QL), BF16),
            pltpu.VMEM((QW, QL), BF16),
            pltpu.VMEM((NOPE, KVL), BF16),
            pltpu.VMEM((KVL, VD), BF16),
            pltpu.VMEM((PAIRS, 2, LLOC, LAT), BF16),
            pltpu.VMEM((N_CTX, ROWS, QW), BF16),
            pltpu.VMEM((N_CTX, ROWS, LAT), BF16),
            pltpu.VMEM((PAIRS, 2, LAT), BF16),
            pltpu.VMEM((N_EXP, 2, LAT), BF16),
            pltpu.VMEM((N_EXP, 2, KVL + 128), BF16),
            pltpu.VMEM((N_EXP, 2, KVL + 128), BF16),
            pltpu.VMEM((N_CTX * N_X, ROWS, VD), BF16),
            pltpu.VMEM((N_X, VD, COLS), BF16),
            pltpu.VMEM((N_Z, 8, COLS), BF16),
            pltpu.VMEM((N_Z, 8, COLS), BF16),
            pltpu.VMEM((8, 1, COLS), F32),
            pltpu.VMEM((8, 1, COLS), F32),
            pltpu.VMEM((N_Z, 2, N_X, COLS), BF16),
            pltpu.VMEM((8, N_Z, N_X, COLS), BF16),
            pltpu.SemaphoreType.DMA((5,)),
            pltpu.SemaphoreType.DMA((3,)),
            pltpu.SemaphoreType.DMA((11,)),
            pltpu.SemaphoreType.DMA((11,)),
            pltpu.SemaphoreType.DMA((N_Z,)),
        ],
        compiler_params=pltpu.CompilerParams(
            collective_id=0, has_side_effects=True, vmem_limit_bytes=60 * 1024 * 1024
        ),
        cost_estimate=pl.CostEstimate(
            flops=600_000_000, bytes_accessed=8_000_000, transcendentals=40_000
        ),
    )(
        owner_slot,
        cached_len,
        owner_slot.reshape(1, N_CTX * ROWS),
        cached_len.reshape(1, N_CTX * ROWS),
        jnp.asarray(half).reshape(1, RD // 2),
        expert_ids.T,
        residual,
        ffn_gain.reshape(1, D),
        prefill_cache,
        query_latent,
        new_latent,
        wq_up.reshape(QL, QW).T,
        wk_up.reshape(NOPE, KVL),
        wv_up.reshape(KVL, VD),
        w_out,
    )
    return hidden, expert_in.reshape(1, 4, CAP, D)


def solution(mesh):
    placed = (
        P("ctx", "exp", None),
        P(),
        P(),
        P("ctx", None),
        P("ctx", None),
        P(None, "exp", None),
        P("exp", None, None),
        P("exp", None, None),
        P("exp", None),
        P(("ctx", "exp"), None),
        P(),
        P("ctx", None),
    )
    return jax.shard_map(
        on_device,
        mesh=mesh,
        in_specs=placed,
        out_specs=(P(("ctx", "exp"), None), P("ctx", "exp", None, None)),
        check_vma=False,
    )
```

```python
import math

import jax
import jax.numpy as jnp
import numpy as np
from jax import lax
from jax.experimental import pallas as pl
from jax.experimental.pallas import tpu as pltpu
from jax.sharding import PartitionSpec as P

MESH = pl.DeviceIdType.MESH
F32 = jnp.float32
BF16 = jnp.bfloat16
N_CTX, N_EXP, N_X, N_Z = 8, 64, 4, 16
ROWS, LLOC, LAT, KVL, NOPE, RD, VD = 64, 8, 576, 512, 128, 64, 128
QL, D, CAP, TOPK, SLOTS = 1536, 7168, 4, 8, 16
QW = NOPE + RD
COLS = D // 8
PAIRS, NEAR = ROWS // 2, N_Z // 2
SCALE = 1.0 / math.sqrt(QW)


def dot(a, b, ca=1, cb=0):
    return lax.dot_general(a, b, (((ca,), (cb,)), ((), ())), preferred_element_type=F32)


def send(src, dst, send_sem, recv_sem, device):
    pltpu.make_async_remote_copy(
        src_ref=src,
        dst_ref=dst,
        send_sem=send_sem,
        recv_sem=recv_sem,
        device_id=device,
        device_id_type=MESH,
    ).start()


def drain(ref, sem):
    pltpu.make_async_copy(ref, ref, sem).wait()


def each(low, high, body):
    def step(k, carry):
        body(k)
        return carry

    lax.fori_loop(low, high, step, 0)


def offset(i, size):
    far = size // 2 - i // 2
    return jnp.where(i % 2 == 0, far, size - far)


def split(value):
    high = value.astype(BF16).astype(F32)
    middle = (value - high).astype(BF16).astype(F32)
    return high, middle, value - high - middle


def one_hot(mask):
    return mask.astype(F32).astype(BF16)


def own_part(row, y, core):
    part = row[:, 0:128]
    for i in range(1, N_CTX // 2):
        part = jnp.where(y == i, row[:, i * 128 : (i + 1) * 128], part)
    return jnp.where(core == 0, part[:, :ROWS], part[:, ROWS:])


def kernel(
    owner_s,
    lens_s,
    owner_row,
    lens_row,
    freqs,
    ids,
    residual,
    gain,
    cache_hbm,
    ql_hbm,
    nl_hbm,
    wq_hbm,
    wk_hbm,
    wv_hbm,
    wo_hbm,
    hidden_ref,
    expert_ref,
    ql,
    wq,
    wk,
    wv,
    kbuf,
    qall,
    nlall,
    qsend,
    qrecv,
    lsend,
    lrecv,
    hsend,
    hall,
    wbuf,
    psend,
    passed,
    psum,
    precv,
    rsend,
    resid,
    other_ids,
    selection,
    zbuf,
    osend,
    orecv,
    slots,
    gbuf,
    load_sem,
    own_sem,
    send_sem,
    recv_sem,
    z_sem,
):
    c = lax.axis_index("ctx")
    e = lax.axis_index("exp")
    y, core = c // 2, lax.rem(c, 2)
    z, x = e // N_X, lax.rem(e, N_X)

    loads = [
        pltpu.make_async_copy(src, dst, load_sem.at[i])
        for i, (src, dst) in enumerate(
            [
                (ql_hbm, ql),
                (wq_hbm, wq),
                (wk_hbm, wk),
                (wv_hbm, wv),
                (nl_hbm, nlall.at[c]),
            ]
        )
    ]
    for load in loads:
        load.start()

    barrier = pltpu.get_barrier_semaphore()
    sent, due = [], {}

    def track(name, ref, i):
        sent.append((ref, send_sem.at[i]))
        due[name] = (ref, recv_sem.at[i])

    def arrive(name):
        drain(*due.pop(name))

    def greet(device):
        pl.semaphore_signal(barrier, inc=1, device_id=device, device_id_type=MESH)

    each(1, N_EXP, lambda k: greet((c, lax.rem(e + k, N_EXP))))

    def greet_plane(k):
        for i in range(N_X):
            greet((lax.rem(c + k, N_CTX), z * N_X + i))

    each(1, N_CTX, greet_plane)

    loads[0].wait()
    loads[1].wait()
    qall[c] = dot(ql[...], wq[...], 1, 1).astype(BF16)
    loads[4].wait()

    pl.semaphore_wait(barrier, N_EXP - 1 + (N_CTX - 1) * N_X)

    def send_q(k):
        to = (lax.rem(c + offset(k, N_CTX), N_CTX), e)
        send(qall.at[c], qall.at[c], send_sem.at[0], recv_sem.at[0], to)

    each(1, N_CTX, send_q)
    track("q", qall.at[pl.ds(0, N_CTX - 1)], 0)

    pair = lax.rem(e, PAIRS)
    own = pltpu.make_async_copy(
        cache_hbm.at[pl.ds(2 * pair, 2)], kbuf.at[NEAR // 2 * N_X + x], recv_sem.at[1]
    )
    own.start()

    def send_cache(i):
        step = i // N_X
        near = NEAR // 2 - (step + 1) // 2
        away = jnp.where(step % 2 == 1, near, N_Z - near)
        away = jnp.where((step == 0) & (z % 2 == 0), NEAR // 2, away)
        to_z = lax.rem(z + away, N_Z)
        to_x = lax.rem(x + i + jnp.where(step == NEAR - 1, 1, 0), N_X)
        into = lax.rem(N_Z - away + NEAR // 2, NEAR) * N_X + x
        pairs = pl.ds(2 * (lax.rem(to_z, NEAR) * N_X + to_x), 2)
        send(cache_hbm.at[pairs], kbuf.at[into], send_sem.at[1], recv_sem.at[1], (c, to_z * N_X + to_x))

    each(0, PAIRS - 1, send_cache)
    sent.append((kbuf.at[pl.ds(0, PAIRS - 1)], send_sem.at[1]))
    due["cache"] = (kbuf, recv_sem.at[1])


    def send_new(k):
        to = (lax.rem(c + offset(k, N_CTX), N_CTX), e)
        send(nlall.at[c], nlall.at[c], send_sem.at[2], recv_sem.at[2], to)

    each(1, N_CTX, send_new)
    track("new", nlall.at[pl.ds(0, N_CTX - 1)], 2)

    mine_row, block = core * N_X + x, x * 2 + core
    for i in range(8):
        rsend[i] = residual[:, i * COLS : (i + 1) * COLS].astype(F32)
    resid[mine_row] = rsend[block]

    def send_residual(k):
        to_x, to_core = lax.rem(x + k // 2, N_X), lax.rem(core + k, 2)
        to = (y * 2 + to_core, z * N_X + to_x)
        send(rsend.at[to_x * 2 + to_core], resid.at[mine_row], send_sem.at[8], recv_sem.at[8], to)

    each(1, 8, send_residual)
    track("residual", resid.at[pl.ds(0, 7)], 8)

    send(ids, other_ids, send_sem.at[11], recv_sem.at[11], (y * 2 + 1 - core, e))
    track("ids", other_ids, 11)

    mine = own_part(owner_row[...], y, core)
    place = (lax.broadcasted_iota(jnp.int32, (N_CTX * ROWS, ROWS), 0) == mine).astype(F32)
    lengths = own_part(lens_row[...], y, core).astype(F32)
    eye = lax.broadcasted_iota(jnp.int32, (ROWS, ROWS), 0) == lax.broadcasted_iota(
        jnp.int32, (ROWS, ROWS), 1
    )
    angles = jnp.sum(jnp.where(eye, lengths, 0.0), 1, keepdims=True) * freqs[...]
    cosines, sines = jnp.cos(angles), jnp.sin(angles)
    loads[2].wait()
    arrive("q")
    q = dot(place.astype(BF16), qall[...].reshape(N_CTX * ROWS, QW), 0, 0)
    absorbed = dot(q[:, :NOPE].astype(BF16), wk[...])
    first, second = q[:, NOPE : NOPE + RD // 2], q[:, NOPE + RD // 2 :]
    turned = jnp.concatenate(
        [first * cosines - second * sines, first * sines + second * cosines], 1
    )
    absorbed = jnp.concatenate([absorbed, turned], 1).astype(BF16)
    qsend[...] = absorbed.reshape(PAIRS, 2, LAT)
    own_query = pltpu.make_async_copy(qsend.at[pair], qrecv.at[e], own_sem.at[1])
    own_query.start()
    due["own_query"] = (qrecv.at[e], own_sem.at[1])

    def send_query(k):
        j = lax.rem(e + offset(k, N_EXP), N_EXP)
        send(qsend.at[lax.rem(j, PAIRS)], qrecv.at[e], send_sem.at[4], recv_sem.at[4], (c, j))

    each(1, N_EXP, send_query)
    track("query", qrecv.at[pl.ds(0, N_EXP - 1)], 4)


    def columns(i):
        return wo_hbm.at[:, pl.ds(pl.multiple_of((i * 2 + core) * COLS, 128), COLS)]

    own_w = pltpu.make_async_copy(columns(x), wbuf.at[x], own_sem.at[0])
    own_w.start()
    due["own_w"] = (wbuf.at[x], own_sem.at[0])

    def send_w(k):
        i = lax.rem(x + k, N_X)
        send(columns(i), wbuf.at[x], send_sem.at[3], recv_sem.at[3], (c, z * N_X + i))

    each(1, N_X, send_w)
    track("w", wbuf.at[pl.ds(0, N_X - 1)], 3)

    arrive("ids")
    earlier = lax.broadcasted_iota(jnp.int32, (ROWS, ROWS), 0) < lax.broadcasted_iota(
        jnp.int32, (ROWS, ROWS), 1
    )
    stage = lax.broadcasted_iota(jnp.int32, (1, ROWS), 1) // N_X
    stage = jnp.where(stage == 0, z, z + N_Z - offset(stage, N_Z)) % N_Z
    held = stage * N_X + lax.broadcasted_iota(jnp.int32, (1, ROWS), 1) % N_X
    held = one_hot(lax.broadcasted_iota(jnp.int32, (ROWS, ROWS), 0) == held)
    expert = z * 16 + lax.broadcasted_iota(jnp.int32, (16, ROWS), 0)
    line = lax.broadcasted_iota(jnp.int32, (ROWS, 16), 0)
    widen = one_hot(line // CAP == lax.broadcasted_iota(jnp.int32, (ROWS, 16), 1))
    slot_of = (lax.broadcasted_iota(jnp.int32, (ROWS, ROWS), 0) % CAP).astype(F32)
    for g in range(2):
        names = jnp.where(core == g, ids[...], other_ids[...])
        named = jnp.zeros((16, ROWS), F32)
        for i in range(TOPK):
            named = named + (names[i : i + 1] == expert).astype(F32)
        named = named.astype(BF16)
        before = dot(named, one_hot(earlier)).astype(BF16)
        taken = (dot(widen, named) > 0.5) & (dot(widen, before) == slot_of)
        selection[g] = dot(one_hot(taken), held).astype(BF16)

    first_request = c * ROWS + 2 * pair
    width = PAIRS * LLOC
    slot = lax.broadcasted_iota(jnp.int32, (1, width), 1) // LLOC
    from_z = z + slot // N_X + N_Z - NEAR // 2
    from_z = jnp.where((slot < N_X) & (z % 2 == 1), z + NEAR // 2, from_z) % N_Z
    position = (from_z * N_X + slot % N_X) * LLOC
    position = position + lax.broadcasted_iota(jnp.int32, (1, width), 1) % LLOC
    even = lax.broadcasted_iota(jnp.int32, (2 * N_EXP, 1), 0) % 2 == 0
    valid = position < jnp.where(even, lens_s[first_request], lens_s[first_request + 1])
    chosen = lax.broadcasted_iota(jnp.int32, (16, 1), 0)
    chosen = jnp.where(chosen == 0, owner_s[first_request], owner_s[first_request + 1])
    pick = (lax.broadcasted_iota(jnp.int32, (16, N_CTX * ROWS), 1) == chosen).astype(F32)
    arrive("new")
    new = dot(pick.astype(BF16), nlall[...].reshape(N_CTX * ROWS, LAT))
    arrive("own_query")
    arrive("query")
    queries = qrecv[...].reshape(2 * N_EXP, LAT)
    new_scores = dot(queries, new.astype(BF16), 1, 1) * SCALE
    new_scores = jnp.where(even, new_scores[:, 0:1], new_scores[:, 1:2])
    new_scores = jnp.where(e < PAIRS, new_scores, -1e30)
    arrive("cache")
    keys = [kbuf[:, t].astype(F32).reshape(width, LAT).astype(BF16) for t in range(2)]
    scores = jnp.where(even, dot(queries, keys[0], 1, 1), dot(queries, keys[1], 1, 1)) * SCALE
    top = jnp.max(jnp.where(valid, scores, -1e30), 1, keepdims=True)
    top = jnp.maximum(top, new_scores)
    weights = jnp.where(valid, jnp.exp(scores - top), 0.0)
    new_weight = jnp.where(e < PAIRS, jnp.exp(new_scores - top), 0.0)
    total = jnp.sum(weights, 1, keepdims=True) + new_weight
    mixed = dot(jnp.where(even, weights, 0.0).astype(BF16), keys[0][:, :KVL])
    mixed = mixed + dot(jnp.where(even, 0.0, weights).astype(BF16), keys[1][:, :KVL])
    mixed = mixed + new_weight.astype(BF16).astype(F32) * jnp.where(
        even, new[0:1, :KVL], new[1:2, :KVL]
    )
    some = total > 0.0
    divisor = jnp.where(some, total, 1.0)
    parts = split(jnp.where(some, top + jnp.log(divisor), -1e30))
    lane = lax.broadcasted_iota(jnp.int32, (2 * N_EXP, 128), 1)
    tail = jnp.zeros((2 * N_EXP, 128), F32)
    for i in range(3):
        tail = jnp.where(lane == i, parts[i], tail)
    latent = jnp.concatenate([mixed / divisor, tail], 1).astype(BF16)
    lsend[...] = latent.reshape(N_EXP, 2, KVL + 128)
    own_latent = pltpu.make_async_copy(lsend.at[e], lrecv.at[e], own_sem.at[2])
    own_latent.start()
    due["own_latent"] = (lrecv.at[e], own_sem.at[2])

    def send_latent(k):
        j = lax.rem(e + offset(k, N_EXP), N_EXP)
        send(lsend.at[j], lrecv.at[e], send_sem.at[5], recv_sem.at[5], (c, j))

    each(1, N_EXP, send_latent)
    track("latent", lrecv.at[pl.ds(0, N_EXP - 1)], 5)

    def ranks(owner):
        rows = jnp.sum(jnp.where(eye, owner, 0.0), 1, keepdims=True)
        return jnp.sum(jnp.where((rows == owner) & earlier, 1.0, 0.0), 0, keepdims=True)

    owner = (mine // ROWS).astype(F32)
    key = (owner * SLOTS + ranks(owner)).astype(jnp.int32)
    bucket = one_hot(lax.broadcasted_iota(jnp.int32, (N_CTX * SLOTS, ROWS), 0) == key)
    keys = []
    for i in range(N_CTX):
        owner = owner_row[:, i * ROWS : (i + 1) * ROWS] // ROWS
        key = (i * 2 + owner - 2 * y) * SLOTS + ranks(owner.astype(F32)).astype(jnp.int32)
        keys.append(jnp.where(owner // 2 == y, key, -1))
    keys = jnp.concatenate(keys, 1)
    keys = one_hot(lax.broadcasted_iota(jnp.int32, (N_CTX * 2 * SLOTS, N_CTX * ROWS), 0) == keys)
    order = lax.broadcasted_iota(jnp.int32, (2 * ROWS, N_CTX * ROWS), 0)
    rest = order % 8
    wanted = (y * 2 + rest // N_X) * ROWS + (order // 8) * N_X + rest % N_X
    place = dot(one_hot(owner_row[...] == wanted), keys, 1, 1).astype(BF16)

    loads[3].wait()
    arrive("own_latent")
    arrive("latent")
    at = c * N_X + x
    halves = lrecv[...].reshape(2 * N_EXP, KVL + 128).astype(F32)
    sums = halves[:, KVL : KVL + 1] + halves[:, KVL + 1 : KVL + 2] + halves[:, KVL + 2 : KVL + 3]
    peak = jnp.maximum(sums[:ROWS], sums[ROWS:])
    low, high = jnp.exp(sums[:ROWS] - peak), jnp.exp(sums[ROWS:] - peak)
    latent = (low * halves[:ROWS, :KVL] + high * halves[ROWS:, :KVL]) / (low + high)
    value = dot(latent.astype(BF16), wv[...]).astype(BF16)
    hsend[...] = dot(bucket, value).astype(BF16).reshape(N_CTX // 2, 2 * SLOTS, VD)
    hall[at] = hsend[y]

    def send_heads(k):
        to_c = lax.rem(c + offset(k, N_CTX), N_CTX)
        for i in range(N_X):
            to = (to_c, z * N_X + lax.rem(x + i, N_X))
            send(hsend.at[to_c // 2], hall.at[at], send_sem.at[6], recv_sem.at[6], to)

    def send_heads_x(k):
        to = (c, z * N_X + lax.rem(x + k, N_X))
        send(hsend.at[y], hall.at[at], send_sem.at[6], recv_sem.at[6], to)

    each(1, N_CTX, send_heads)
    each(1, N_X, send_heads_x)
    track("heads", hall.at[pl.ds(0, N_CTX * N_X - 1)], 6)

    arrive("own_w")
    arrive("w")
    arrive("heads")
    partial = jnp.zeros((2 * ROWS, COLS), F32)
    heads = hall[...].reshape(N_CTX, N_X, 2 * SLOTS, VD)
    for i in range(N_X):
        head = dot(place, heads[:, i].reshape(N_CTX * 2 * SLOTS, VD)).astype(BF16)
        partial = partial + dot(head, wbuf[i])
    psend[...] = partial.reshape(N_Z, 8, COLS).astype(BF16)
    precv[4] = psend[z]

    def at_z(hop):
        return lax.rem(z + hop + N_Z, N_Z)

    def along_z(source, into, hop, recv):
        send(source, into, send_sem.at[7], recv, (c, at_z(hop) * N_X + x))

    for j in range(3):
        along_z(psend.at[at_z(-5 - j)], passed.at[0, j], -1 - j, z_sem.at[0])
        along_z(psend.at[at_z(5 + j)], passed.at[1, j], 1 + j, z_sem.at[1])

    @pl.when(z % 2 == 0)
    def _():
        along_z(psend.at[at_z(8)], passed.at[0, 3], -4, z_sem.at[2])

    @pl.when(z % 2 == 1)
    def _():
        along_z(psend.at[at_z(8)], passed.at[1, 3], 4, z_sem.at[2])

    for j in range(1, 4):
        along_z(psend.at[at_z(j)], precv.at[4 - j], j, recv_sem.at[7])
        along_z(psend.at[at_z(-j)], precv.at[4 + j], -j, recv_sem.at[7])
    for side in range(2):
        drain(passed.at[side, pl.ds(0, 3)], z_sem.at[side])
        hop = -4 if side == 0 else 4
        through = psend[at_z(hop)].astype(F32)
        for j in range(3):
            through = through + passed[side, j].astype(F32)
        psum[side] = through.astype(BF16)

        @pl.when(z % 2 == side)
        def _():
            drain(passed.at[side, 3], z_sem.at[2])
            psum[side] = (through + passed[side, 3].astype(F32)).astype(BF16)

        along_z(psum.at[side], precv.at[4 - hop], hop, recv_sem.at[7])
    sent.append((psend.at[pl.ds(0, N_Z - 1)], send_sem.at[7]))
    due["partial"] = (precv.at[pl.ds(0, 8)], recv_sem.at[7])
    arrive("partial")
    summed = precv[0].astype(F32)
    for i in range(1, 9):
        summed = summed + precv[i].astype(F32)

    arrive("residual")
    hidden = summed + resid[:, 0, :]
    zbuf[0] = hidden.astype(BF16).reshape(2, N_X, COLS)

    def pass_on(source, into, hop, recv):
        send(zbuf.at[source], zbuf.at[into], send_sem.at[9], recv, (c, at_z(hop) * N_X + x))

    pass_on(0, 8, 4, z_sem.at[3])
    pass_on(0, 9, -4, z_sem.at[4])
    for j in range(1, 4):
        pass_on(0, 16 - 2 * j, j, recv_sem.at[9])
        pass_on(0, 17 - 2 * j, -j, recv_sem.at[9])

    osend[:, 0, :] = hidden
    orecv[block] = osend[mine_row]

    def send_row(k):
        to_x, to_core = lax.rem(x + k // 2, N_X), lax.rem(core + k, 2)
        to = (y * 2 + to_core, z * N_X + to_x)
        send(osend.at[to_core * N_X + to_x], orecv.at[block], send_sem.at[12], recv_sem.at[12], to)

    each(1, 8, send_row)
    track("row", orecv.at[pl.ds(0, 7)], 12)

    for side in range(2):
        drain(zbuf.at[8 + side], z_sem.at[3 + side])
        way = 1 - 2 * side

        @pl.when(z % 2 == side)
        def _():
            pass_on(8 + side, 1, 4 * way, recv_sem.at[9])

        for j in range(3):
            pass_on(8 + side, 2 + 2 * j + side, (3 - j) * way, recv_sem.at[9])
    sent.append((zbuf.at[pl.ds(0, N_Z - 1)], send_sem.at[9]))
    due["columns"] = (zbuf.at[pl.ds(0, N_Z - 3)], recv_sem.at[9])

    arrive("columns")
    for g in range(2):
        rows = dot(selection[g], zbuf[:, g].reshape(ROWS, COLS)).astype(BF16)
        slots[g] = rows.reshape(N_X, 16, COLS)

    def send_slots(k):
        to_x, to_core = lax.rem(x + k // 2, N_X), lax.rem(core + k, 2)
        to = (y * 2 + to_core, z * N_X + to_x)
        send(slots.at[to_core, to_x], gbuf.at[block], send_sem.at[10], recv_sem.at[10], to)

    each(1, 8, send_slots)
    track("slots", gbuf.at[pl.ds(0, 7)], 10)
    gbuf[block] = slots[core, x]
    arrive("row")
    for i in range(8):
        hidden_ref[:, i * COLS : (i + 1) * COLS] = orecv[i].astype(BF16)
    arrive("slots")

    square = jnp.zeros((16, 1), F32)
    for i in range(8):
        rows = gbuf[i].astype(F32)
        square = square + jnp.sum(rows * rows, 1, keepdims=True)
    factor = lax.rsqrt(square * (1.0 / D) + 1e-06)
    for i in range(8):
        there = slice(i * COLS, (i + 1) * COLS)
        expert_ref[:, there] = (gbuf[i].astype(F32) * factor * gain[:, there]).astype(BF16)

    for ref, sem in sent:
        drain(ref, sem)


def place_results(hidden, expert_in, hidden_ref, expert_ref):
    hidden_ref[...] = hidden[...]
    for i in range(4):
        expert_ref[0, i] = expert_in[i * CAP : (i + 1) * CAP]


def on_device(
    prefill_cache,
    owner_slot,
    cached_len,
    query_latent,
    new_latent,
    wq_up,
    wk_up,
    wv_up,
    w_out,
    residual,
    ffn_gain,
    expert_ids,
):
    half = (10000.0 ** (-2.0 * np.arange(RD // 2, dtype=np.float32) / RD)).astype(np.float32)
    smem = pl.BlockSpec(memory_space=pltpu.SMEM)
    vmem = pl.BlockSpec(memory_space=pltpu.VMEM)
    anywhere = pl.BlockSpec(memory_space=pl.ANY)
    hidden, expert_in = pl.pallas_call(
        kernel,
        out_shape=(
            jax.ShapeDtypeStruct((1, D), BF16),
            jax.ShapeDtypeStruct((4 * CAP, D), BF16),
        ),
        in_specs=[smem] * 2 + [vmem] * 6 + [anywhere] * 7,
        out_specs=(vmem, vmem),
        scratch_shapes=[
            pltpu.VMEM((ROWS, QL), BF16),
            pltpu.VMEM((QW, QL), BF16),
            pltpu.VMEM((NOPE, KVL), BF16),
            pltpu.VMEM((KVL, VD), BF16),
            pltpu.VMEM((PAIRS, 2, LLOC, LAT), BF16),
            pltpu.VMEM((N_CTX, ROWS, QW), BF16),
            pltpu.VMEM((N_CTX, ROWS, LAT), BF16),
            pltpu.VMEM((PAIRS, 2, LAT), BF16),
            pltpu.VMEM((N_EXP, 2, LAT), BF16),
            pltpu.VMEM((N_EXP, 2, KVL + 128), BF16),
            pltpu.VMEM((N_EXP, 2, KVL + 128), BF16),
            pltpu.VMEM((N_CTX // 2, 2 * SLOTS, VD), BF16),
            pltpu.VMEM((N_CTX * N_X, 2 * SLOTS, VD), BF16),
            pltpu.VMEM((N_X, VD, COLS), BF16),
            pltpu.VMEM((N_Z, 8, COLS), BF16),
            pltpu.VMEM((2, 4, 8, COLS), BF16),
            pltpu.VMEM((2, 8, COLS), BF16),
            pltpu.VMEM((9, 8, COLS), BF16),
            pltpu.VMEM((8, 1, COLS), F32),
            pltpu.VMEM((8, 1, COLS), F32),
            pltpu.VMEM((TOPK, ROWS), jnp.int32),
            pltpu.VMEM((2, ROWS, ROWS), BF16),
            pltpu.VMEM((N_Z, 2, N_X, COLS), BF16),
            pltpu.VMEM((8, 1, COLS), F32),
            pltpu.VMEM((8, 1, COLS), F32),
            pltpu.VMEM((2, N_X, 16, COLS), BF16),
            pltpu.VMEM((8, 16, COLS), BF16),
            pltpu.SemaphoreType.DMA((5,)),
            pltpu.SemaphoreType.DMA((3,)),
            pltpu.SemaphoreType.DMA((13,)),
            pltpu.SemaphoreType.DMA((13,)),
            pltpu.SemaphoreType.DMA((5,)),
        ],
        compiler_params=pltpu.CompilerParams(
            collective_id=0, has_side_effects=True, vmem_limit_bytes=60 * 1024 * 1024
        ),
        cost_estimate=pl.CostEstimate(
            flops=600_000_000, bytes_accessed=8_000_000, transcendentals=40_000
        ),
    )(
        owner_slot,
        cached_len,
        owner_slot.reshape(1, N_CTX * ROWS),
        cached_len.reshape(1, N_CTX * ROWS),
        jnp.asarray(half).reshape(1, RD // 2),
        expert_ids.T,
        residual,
        ffn_gain.reshape(1, D),
        prefill_cache,
        query_latent,
        new_latent,
        wq_up.reshape(QL, QW).T,
        wk_up.reshape(NOPE, KVL),
        wv_up.reshape(KVL, VD),
        w_out,
    )
    return pl.pallas_call(
        place_results,
        out_shape=(
            jax.ShapeDtypeStruct((1, D), BF16),
            jax.ShapeDtypeStruct((1, 4, CAP, D), BF16),
        ),
        in_specs=[vmem] * 2,
        out_specs=(vmem, vmem),
    )(hidden, expert_in)


def solution(mesh):
    placed = (
        P("ctx", "exp", None),
        P(),
        P(),
        P("ctx", None),
        P("ctx", None),
        P(None, "exp", None),
        P("exp", None, None),
        P("exp", None, None),
        P("exp", None),
        P(("ctx", "exp"), None),
        P(),
        P("ctx", None),
    )
    return jax.shard_map(
        on_device,
        mesh=mesh,
        in_specs=placed,
        out_specs=(P(("ctx", "exp"), None), P("ctx", "exp", None, None)),
        check_vma=False,
    )
```

```python
import math

import jax
import jax.numpy as jnp
import numpy as np
from jax import lax
from jax.experimental import pallas as pl
from jax.experimental.pallas import tpu as pltpu
from jax.sharding import PartitionSpec as P

MESH = pl.DeviceIdType.MESH
F32 = jnp.float32
BF16 = jnp.bfloat16
N_CTX, N_EXP, N_X, N_Z = 8, 64, 4, 16
ROWS, LLOC, LAT, KVL, NOPE, RD, VD = 64, 8, 576, 512, 128, 64, 128
QL, D, CAP, TOPK, SLOTS = 1536, 7168, 4, 8, 16
QW = NOPE + RD
COLS = D // 8
PAIRS, NEAR = ROWS // 2, N_Z // 2
SCALE = 1.0 / math.sqrt(QW)


def dot(a, b, ca=1, cb=0):
    return lax.dot_general(a, b, (((ca,), (cb,)), ((), ())), preferred_element_type=F32)


def send(src, dst, send_sem, recv_sem, device):
    pltpu.make_async_remote_copy(
        src_ref=src,
        dst_ref=dst,
        send_sem=send_sem,
        recv_sem=recv_sem,
        device_id=device,
        device_id_type=MESH,
    ).start()


def drain(ref, sem):
    pltpu.make_async_copy(ref, ref, sem).wait()


def each(low, high, body):
    def step(k, carry):
        body(k)
        return carry

    lax.fori_loop(low, high, step, 0)


def offset(i, size):
    far = size // 2 - i // 2
    return jnp.where(i % 2 == 0, far, size - far)


def split(value):
    high = value.astype(BF16).astype(F32)
    middle = (value - high).astype(BF16).astype(F32)
    return high, middle, value - high - middle


def one_hot(mask):
    return mask.astype(F32).astype(BF16)


def own_part(row, y, core):
    part = row[:, 0:128]
    for i in range(1, N_CTX // 2):
        part = jnp.where(y == i, row[:, i * 128 : (i + 1) * 128], part)
    return jnp.where(core == 0, part[:, :ROWS], part[:, ROWS:])


def kernel(
    owner_s,
    lens_s,
    owner_row,
    lens_row,
    freqs,
    ids,
    residual,
    gain,
    cache_hbm,
    ql_hbm,
    nl_hbm,
    wq_hbm,
    wk_hbm,
    wv_hbm,
    wo_hbm,
    hidden_ref,
    expert_ref,
    ql,
    wq,
    wk,
    wv,
    stage,
    ropes,
    kbuf,
    rbuf,
    qall,
    nlall,
    qsend,
    qrecv,
    lsend,
    lrecv,
    hsend,
    hall,
    wbuf,
    psend,
    passed,
    psum,
    precv,
    rsend,
    resid,
    other_ids,
    selection,
    zbuf,
    osend,
    orecv,
    slots,
    gbuf,
    load_sem,
    own_sem,
    send_sem,
    recv_sem,
    z_sem,
):
    c = lax.axis_index("ctx")
    e = lax.axis_index("exp")
    y, core = c // 2, lax.rem(c, 2)
    z, x = e // N_X, lax.rem(e, N_X)

    loads = [
        pltpu.make_async_copy(src, dst, load_sem.at[i])
        for i, (src, dst) in enumerate(
            [
                (ql_hbm, ql),
                (wq_hbm, wq),
                (wk_hbm, wk),
                (wv_hbm, wv),
                (nl_hbm, nlall.at[c]),
                (cache_hbm.at[:, :, pl.ds(KVL, RD)], stage),
            ]
        )
    ]
    for load in loads:
        load.start()

    barrier = pltpu.get_barrier_semaphore()
    sent, due = [], {}

    def track(name, ref, i):
        sent.append((ref, send_sem.at[i]))
        due[name] = (ref, recv_sem.at[i])

    def arrive(name):
        drain(*due.pop(name))

    def greet(device):
        pl.semaphore_signal(barrier, inc=1, device_id=device, device_id_type=MESH)

    each(1, N_EXP, lambda k: greet((c, lax.rem(e + k, N_EXP))))

    def greet_plane(k):
        for i in range(N_X):
            greet((lax.rem(c + k, N_CTX), z * N_X + i))

    each(1, N_CTX, greet_plane)

    loads[0].wait()
    loads[1].wait()
    qall[c] = dot(ql[...], wq[...], 1, 1).astype(BF16)
    loads[4].wait()
    loads[5].wait()
    parts = stage[...].astype(F32).reshape(PAIRS, 2, LLOC, RD)
    ropes[...] = jnp.concatenate([parts[:, 0], parts[:, 1]], 2).astype(BF16)

    pl.semaphore_wait(barrier, N_EXP - 1 + (N_CTX - 1) * N_X)

    def send_q(k):
        to = (lax.rem(c + offset(k, N_CTX), N_CTX), e)
        send(qall.at[c], qall.at[c], send_sem.at[0], recv_sem.at[0], to)

    each(1, N_CTX, send_q)
    track("q", qall.at[pl.ds(0, N_CTX - 1)], 0)

    pair = lax.rem(e, PAIRS)
    def latents(first):
        return cache_hbm.at[pl.ds(2 * first, 2), :, pl.ds(0, KVL)]

    home = NEAR // 2 * N_X + x
    own = [
        pltpu.make_async_copy(latents(pair), kbuf.at[home], recv_sem.at[1]),
        pltpu.make_async_copy(ropes.at[pair], rbuf.at[home], recv_sem.at[13]),
    ]
    for copy in own:
        copy.start()

    def send_cache(i):
        step = i // N_X
        near = NEAR // 2 - (step + 1) // 2
        away = jnp.where(step % 2 == 1, near, N_Z - near)
        away = jnp.where((step == 0) & (z % 2 == 0), NEAR // 2, away)
        to_z = lax.rem(z + away, N_Z)
        to_x = lax.rem(x + i + jnp.where(step == NEAR - 1, 1, 0), N_X)
        into = lax.rem(N_Z - away + NEAR // 2, NEAR) * N_X + x
        first = lax.rem(to_z, NEAR) * N_X + to_x
        to = (c, to_z * N_X + to_x)
        send(latents(first), kbuf.at[into], send_sem.at[1], recv_sem.at[1], to)
        send(ropes.at[first], rbuf.at[into], send_sem.at[13], recv_sem.at[13], to)

    each(0, PAIRS - 1, send_cache)
    sent.append((kbuf.at[pl.ds(0, PAIRS - 1)], send_sem.at[1]))
    due["cache"] = (kbuf, recv_sem.at[1])
    sent.append((rbuf.at[pl.ds(0, PAIRS - 1)], send_sem.at[13]))
    due["ropes"] = (rbuf, recv_sem.at[13])


    def send_new(k):
        to = (lax.rem(c + offset(k, N_CTX), N_CTX), e)
        send(nlall.at[c], nlall.at[c], send_sem.at[2], recv_sem.at[2], to)

    each(1, N_CTX, send_new)
    track("new", nlall.at[pl.ds(0, N_CTX - 1)], 2)

    mine_row, block = core * N_X + x, x * 2 + core
    for i in range(8):
        rsend[i] = residual[:, i * COLS : (i + 1) * COLS].astype(F32)
    resid[mine_row] = rsend[block]

    def send_residual(k):
        to_x, to_core = lax.rem(x + k // 2, N_X), lax.rem(core + k, 2)
        to = (y * 2 + to_core, z * N_X + to_x)
        send(rsend.at[to_x * 2 + to_core], resid.at[mine_row], send_sem.at[8], recv_sem.at[8], to)

    each(1, 8, send_residual)
    track("residual", resid.at[pl.ds(0, 7)], 8)

    send(ids, other_ids, send_sem.at[11], recv_sem.at[11], (y * 2 + 1 - core, e))
    track("ids", other_ids, 11)

    mine = own_part(owner_row[...], y, core)
    place = (lax.broadcasted_iota(jnp.int32, (N_CTX * ROWS, ROWS), 0) == mine).astype(F32)
    lengths = own_part(lens_row[...], y, core).astype(F32)
    eye = lax.broadcasted_iota(jnp.int32, (ROWS, ROWS), 0) == lax.broadcasted_iota(
        jnp.int32, (ROWS, ROWS), 1
    )
    angles = jnp.sum(jnp.where(eye, lengths, 0.0), 1, keepdims=True) * freqs[...]
    cosines, sines = jnp.cos(angles), jnp.sin(angles)
    loads[2].wait()
    arrive("q")
    q = dot(place.astype(BF16), qall[...].reshape(N_CTX * ROWS, QW), 0, 0)
    absorbed = dot(q[:, :NOPE].astype(BF16), wk[...])
    first, second = q[:, NOPE : NOPE + RD // 2], q[:, NOPE + RD // 2 :]
    turned = jnp.concatenate(
        [first * cosines - second * sines, first * sines + second * cosines], 1
    )
    absorbed = jnp.concatenate([absorbed, turned], 1).astype(BF16)
    qsend[...] = absorbed.reshape(PAIRS, 2, LAT)
    own_query = pltpu.make_async_copy(qsend.at[pair], qrecv.at[e], own_sem.at[1])
    own_query.start()
    due["own_query"] = (qrecv.at[e], own_sem.at[1])

    def send_query(k):
        j = lax.rem(e + offset(k, N_EXP), N_EXP)
        send(qsend.at[lax.rem(j, PAIRS)], qrecv.at[e], send_sem.at[4], recv_sem.at[4], (c, j))

    each(1, N_EXP, send_query)
    track("query", qrecv.at[pl.ds(0, N_EXP - 1)], 4)


    def columns(i):
        return wo_hbm.at[:, pl.ds(pl.multiple_of((i * 2 + core) * COLS, 128), COLS)]

    own_w = pltpu.make_async_copy(columns(x), wbuf.at[x], own_sem.at[0])
    own_w.start()
    due["own_w"] = (wbuf.at[x], own_sem.at[0])

    def send_w(k):
        i = lax.rem(x + k, N_X)
        send(columns(i), wbuf.at[x], send_sem.at[3], recv_sem.at[3], (c, z * N_X + i))

    each(1, N_X, send_w)
    track("w", wbuf.at[pl.ds(0, N_X - 1)], 3)

    arrive("ids")
    earlier = lax.broadcasted_iota(jnp.int32, (ROWS, ROWS), 0) < lax.broadcasted_iota(
        jnp.int32, (ROWS, ROWS), 1
    )
    turn = lax.broadcasted_iota(jnp.int32, (1, ROWS), 1) // N_X
    turn = jnp.where(turn == 0, z, z + N_Z - offset(turn, N_Z)) % N_Z
    held = turn * N_X + lax.broadcasted_iota(jnp.int32, (1, ROWS), 1) % N_X
    held = one_hot(lax.broadcasted_iota(jnp.int32, (ROWS, ROWS), 0) == held)
    expert = z * 16 + lax.broadcasted_iota(jnp.int32, (16, ROWS), 0)
    line = lax.broadcasted_iota(jnp.int32, (ROWS, 16), 0)
    widen = one_hot(line // CAP == lax.broadcasted_iota(jnp.int32, (ROWS, 16), 1))
    slot_of = (lax.broadcasted_iota(jnp.int32, (ROWS, ROWS), 0) % CAP).astype(F32)
    for g in range(2):
        names = jnp.where(core == g, ids[...], other_ids[...])
        named = jnp.zeros((16, ROWS), F32)
        for i in range(TOPK):
            named = named + (names[i : i + 1] == expert).astype(F32)
        named = named.astype(BF16)
        before = dot(named, one_hot(earlier)).astype(BF16)
        taken = (dot(widen, named) > 0.5) & (dot(widen, before) == slot_of)
        selection[g] = dot(one_hot(taken), held).astype(BF16)

    first_request = c * ROWS + 2 * pair
    width = PAIRS * LLOC
    slot = lax.broadcasted_iota(jnp.int32, (1, width), 1) // LLOC
    from_z = z + slot // N_X + N_Z - NEAR // 2
    from_z = jnp.where((slot < N_X) & (z % 2 == 1), z + NEAR // 2, from_z) % N_Z
    position = (from_z * N_X + slot % N_X) * LLOC
    position = position + lax.broadcasted_iota(jnp.int32, (1, width), 1) % LLOC
    even = lax.broadcasted_iota(jnp.int32, (2 * N_EXP, 1), 0) % 2 == 0
    valid = position < jnp.where(even, lens_s[first_request], lens_s[first_request + 1])
    chosen = lax.broadcasted_iota(jnp.int32, (16, 1), 0)
    chosen = jnp.where(chosen == 0, owner_s[first_request], owner_s[first_request + 1])
    pick = (lax.broadcasted_iota(jnp.int32, (16, N_CTX * ROWS), 1) == chosen).astype(F32)
    arrive("new")
    new = dot(pick.astype(BF16), nlall[...].reshape(N_CTX * ROWS, LAT))
    arrive("cache")
    arrive("ropes")
    keys = [kbuf[:, t].astype(F32).reshape(width, KVL).astype(BF16) for t in range(2)]
    turned_keys = rbuf[...].astype(F32).reshape(width, 2 * RD).astype(BF16)
    half = lax.broadcasted_iota(jnp.int32, (2 * N_EXP, 2 * RD), 1) < RD
    arrive("own_query")
    arrive("query")
    queries = qrecv[...].reshape(2 * N_EXP, LAT)
    new_scores = dot(queries, new.astype(BF16), 1, 1) * SCALE
    new_scores = jnp.where(even, new_scores[:, 0:1], new_scores[:, 1:2])
    new_scores = jnp.where(e < PAIRS, new_scores, -1e30)
    latent_part = queries[:, :KVL]
    turned_part = queries[:, KVL:].astype(F32)
    turned_part = jnp.concatenate([turned_part, turned_part], 1)
    turned_part = jnp.where(half == even, turned_part, 0.0).astype(BF16)
    scores = jnp.where(even, dot(latent_part, keys[0], 1, 1), dot(latent_part, keys[1], 1, 1))
    scores = (scores + dot(turned_part, turned_keys, 1, 1)) * SCALE
    top = jnp.max(jnp.where(valid, scores, -1e30), 1, keepdims=True)
    top = jnp.maximum(top, new_scores)
    weights = jnp.where(valid, jnp.exp(scores - top), 0.0)
    new_weight = jnp.where(e < PAIRS, jnp.exp(new_scores - top), 0.0)
    total = jnp.sum(weights, 1, keepdims=True) + new_weight
    mixed = dot(jnp.where(even, weights, 0.0).astype(BF16), keys[0])
    mixed = mixed + dot(jnp.where(even, 0.0, weights).astype(BF16), keys[1])
    mixed = mixed + new_weight.astype(BF16).astype(F32) * jnp.where(
        even, new[0:1, :KVL], new[1:2, :KVL]
    )
    some = total > 0.0
    divisor = jnp.where(some, total, 1.0)
    parts = split(jnp.where(some, top + jnp.log(divisor), -1e30))
    lane = lax.broadcasted_iota(jnp.int32, (2 * N_EXP, 128), 1)
    tail = jnp.zeros((2 * N_EXP, 128), F32)
    for i in range(3):
        tail = jnp.where(lane == i, parts[i], tail)
    latent = jnp.concatenate([mixed / divisor, tail], 1).astype(BF16)
    lsend[...] = latent.reshape(N_EXP, 2, KVL + 128)
    own_latent = pltpu.make_async_copy(lsend.at[e], lrecv.at[e], own_sem.at[2])
    own_latent.start()
    due["own_latent"] = (lrecv.at[e], own_sem.at[2])

    def send_latent(k):
        j = lax.rem(e + offset(k, N_EXP), N_EXP)
        send(lsend.at[j], lrecv.at[e], send_sem.at[5], recv_sem.at[5], (c, j))

    each(1, N_EXP, send_latent)
    track("latent", lrecv.at[pl.ds(0, N_EXP - 1)], 5)

    def ranks(owner):
        rows = jnp.sum(jnp.where(eye, owner, 0.0), 1, keepdims=True)
        return jnp.sum(jnp.where((rows == owner) & earlier, 1.0, 0.0), 0, keepdims=True)

    owner = (mine // ROWS).astype(F32)
    key = (owner * SLOTS + ranks(owner)).astype(jnp.int32)
    bucket = one_hot(lax.broadcasted_iota(jnp.int32, (N_CTX * SLOTS, ROWS), 0) == key)
    keys = []
    for i in range(N_CTX):
        owner = owner_row[:, i * ROWS : (i + 1) * ROWS] // ROWS
        key = (i * 2 + owner - 2 * y) * SLOTS + ranks(owner.astype(F32)).astype(jnp.int32)
        keys.append(jnp.where(owner // 2 == y, key, -1))
    keys = jnp.concatenate(keys, 1)
    keys = one_hot(lax.broadcasted_iota(jnp.int32, (N_CTX * 2 * SLOTS, N_CTX * ROWS), 0) == keys)
    order = lax.broadcasted_iota(jnp.int32, (2 * ROWS, N_CTX * ROWS), 0)
    rest = order % 8
    wanted = (y * 2 + rest // N_X) * ROWS + (order // 8) * N_X + rest % N_X
    place = dot(one_hot(owner_row[...] == wanted), keys, 1, 1).astype(BF16)

    loads[3].wait()
    arrive("own_latent")
    arrive("latent")
    at = c * N_X + x
    halves = lrecv[...].reshape(2 * N_EXP, KVL + 128).astype(F32)
    sums = halves[:, KVL : KVL + 1] + halves[:, KVL + 1 : KVL + 2] + halves[:, KVL + 2 : KVL + 3]
    peak = jnp.maximum(sums[:ROWS], sums[ROWS:])
    low, high = jnp.exp(sums[:ROWS] - peak), jnp.exp(sums[ROWS:] - peak)
    latent = (low * halves[:ROWS, :KVL] + high * halves[ROWS:, :KVL]) / (low + high)
    value = dot(latent.astype(BF16), wv[...]).astype(BF16)
    hsend[...] = dot(bucket, value).astype(BF16).reshape(N_CTX // 2, 2 * SLOTS, VD)
    hall[at] = hsend[y]

    def send_heads(k):
        to_c = lax.rem(c + offset(k, N_CTX), N_CTX)
        for i in range(N_X):
            to = (to_c, z * N_X + lax.rem(x + i, N_X))
            send(hsend.at[to_c // 2], hall.at[at], send_sem.at[6], recv_sem.at[6], to)

    def send_heads_x(k):
        to = (c, z * N_X + lax.rem(x + k, N_X))
        send(hsend.at[y], hall.at[at], send_sem.at[6], recv_sem.at[6], to)

    each(1, N_CTX, send_heads)
    each(1, N_X, send_heads_x)
    track("heads", hall.at[pl.ds(0, N_CTX * N_X - 1)], 6)

    arrive("own_w")
    arrive("w")
    arrive("heads")
    partial = jnp.zeros((2 * ROWS, COLS), F32)
    heads = hall[...].reshape(N_CTX, N_X, 2 * SLOTS, VD)
    for i in range(N_X):
        head = dot(place, heads[:, i].reshape(N_CTX * 2 * SLOTS, VD)).astype(BF16)
        partial = partial + dot(head, wbuf[i])
    psend[...] = partial.reshape(N_Z, 8, COLS).astype(BF16)
    precv[4] = psend[z]

    def at_z(hop):
        return lax.rem(z + hop + N_Z, N_Z)

    def along_z(source, into, hop, recv):
        send(source, into, send_sem.at[7], recv, (c, at_z(hop) * N_X + x))

    for j in range(3):
        along_z(psend.at[at_z(-5 - j)], passed.at[0, j], -1 - j, z_sem.at[0])
        along_z(psend.at[at_z(5 + j)], passed.at[1, j], 1 + j, z_sem.at[1])

    @pl.when(z % 2 == 0)
    def _():
        along_z(psend.at[at_z(8)], passed.at[0, 3], -4, z_sem.at[2])

    @pl.when(z % 2 == 1)
    def _():
        along_z(psend.at[at_z(8)], passed.at[1, 3], 4, z_sem.at[2])

    for j in range(1, 4):
        along_z(psend.at[at_z(j)], precv.at[4 - j], j, recv_sem.at[7])
        along_z(psend.at[at_z(-j)], precv.at[4 + j], -j, recv_sem.at[7])
    for side in range(2):
        drain(passed.at[side, pl.ds(0, 3)], z_sem.at[side])
        hop = -4 if side == 0 else 4
        through = psend[at_z(hop)].astype(F32)
        for j in range(3):
            through = through + passed[side, j].astype(F32)
        psum[side] = through.astype(BF16)

        @pl.when(z % 2 == side)
        def _():
            drain(passed.at[side, 3], z_sem.at[2])
            psum[side] = (through + passed[side, 3].astype(F32)).astype(BF16)

        along_z(psum.at[side], precv.at[4 - hop], hop, recv_sem.at[7])
    sent.append((psend.at[pl.ds(0, N_Z - 1)], send_sem.at[7]))
    due["partial"] = (precv.at[pl.ds(0, 8)], recv_sem.at[7])
    arrive("partial")
    summed = precv[0].astype(F32)
    for i in range(1, 9):
        summed = summed + precv[i].astype(F32)

    arrive("residual")
    hidden = summed + resid[:, 0, :]
    zbuf[0] = hidden.astype(BF16).reshape(2, N_X, COLS)

    def pass_on(source, into, hop, recv):
        send(zbuf.at[source], zbuf.at[into], send_sem.at[9], recv, (c, at_z(hop) * N_X + x))

    pass_on(0, 8, 4, z_sem.at[3])
    pass_on(0, 9, -4, z_sem.at[4])
    for j in range(1, 4):
        pass_on(0, 16 - 2 * j, j, recv_sem.at[9])
        pass_on(0, 17 - 2 * j, -j, recv_sem.at[9])

    osend[:, 0, :] = hidden
    orecv[block] = osend[mine_row]

    def send_row(k):
        to_x, to_core = lax.rem(x + k // 2, N_X), lax.rem(core + k, 2)
        to = (y * 2 + to_core, z * N_X + to_x)
        send(osend.at[to_core * N_X + to_x], orecv.at[block], send_sem.at[12], recv_sem.at[12], to)

    each(1, 8, send_row)
    track("row", orecv.at[pl.ds(0, 7)], 12)

    for side in range(2):
        drain(zbuf.at[8 + side], z_sem.at[3 + side])
        way = 1 - 2 * side

        @pl.when(z % 2 == side)
        def _():
            pass_on(8 + side, 1, 4 * way, recv_sem.at[9])

        for j in range(3):
            pass_on(8 + side, 2 + 2 * j + side, (3 - j) * way, recv_sem.at[9])
    sent.append((zbuf.at[pl.ds(0, N_Z - 1)], send_sem.at[9]))
    due["columns"] = (zbuf.at[pl.ds(0, N_Z - 3)], recv_sem.at[9])

    arrive("columns")
    for g in range(2):
        rows = dot(selection[g], zbuf[:, g].reshape(ROWS, COLS)).astype(BF16)
        slots[g] = rows.reshape(N_X, 16, COLS)

    def send_slots(k):
        to_x, to_core = lax.rem(x + k // 2, N_X), lax.rem(core + k, 2)
        to = (y * 2 + to_core, z * N_X + to_x)
        send(slots.at[to_core, to_x], gbuf.at[block], send_sem.at[10], recv_sem.at[10], to)

    each(1, 8, send_slots)
    track("slots", gbuf.at[pl.ds(0, 7)], 10)
    gbuf[block] = slots[core, x]
    arrive("row")
    for i in range(8):
        hidden_ref[:, i * COLS : (i + 1) * COLS] = orecv[i].astype(BF16)
    arrive("slots")

    square = jnp.zeros((16, 1), F32)
    for i in range(8):
        rows = gbuf[i].astype(F32)
        square = square + jnp.sum(rows * rows, 1, keepdims=True)
    factor = lax.rsqrt(square * (1.0 / D) + 1e-06)
    for i in range(8):
        there = slice(i * COLS, (i + 1) * COLS)
        expert_ref[:, there] = (gbuf[i].astype(F32) * factor * gain[:, there]).astype(BF16)

    for ref, sem in sent:
        drain(ref, sem)


def place_results(hidden, expert_in, hidden_ref, expert_ref):
    hidden_ref[...] = hidden[...]
    for i in range(4):
        expert_ref[0, i] = expert_in[i * CAP : (i + 1) * CAP]


def on_device(
    prefill_cache,
    owner_slot,
    cached_len,
    query_latent,
    new_latent,
    wq_up,
    wk_up,
    wv_up,
    w_out,
    residual,
    ffn_gain,
    expert_ids,
):
    half = (10000.0 ** (-2.0 * np.arange(RD // 2, dtype=np.float32) / RD)).astype(np.float32)
    smem = pl.BlockSpec(memory_space=pltpu.SMEM)
    vmem = pl.BlockSpec(memory_space=pltpu.VMEM)
    anywhere = pl.BlockSpec(memory_space=pl.ANY)
    hidden, expert_in = pl.pallas_call(
        kernel,
        out_shape=(
            jax.ShapeDtypeStruct((1, D), BF16),
            jax.ShapeDtypeStruct((4 * CAP, D), BF16),
        ),
        in_specs=[smem] * 2 + [vmem] * 6 + [anywhere] * 7,
        out_specs=(vmem, vmem),
        scratch_shapes=[
            pltpu.VMEM((ROWS, QL), BF16),
            pltpu.VMEM((QW, QL), BF16),
            pltpu.VMEM((NOPE, KVL), BF16),
            pltpu.VMEM((KVL, VD), BF16),
            pltpu.VMEM((N_EXP, LLOC, RD), BF16),
            pltpu.VMEM((PAIRS, LLOC, 2 * RD), BF16),
            pltpu.VMEM((PAIRS, 2, LLOC, KVL), BF16),
            pltpu.VMEM((PAIRS, LLOC, 2 * RD), BF16),
            pltpu.VMEM((N_CTX, ROWS, QW), BF16),
            pltpu.VMEM((N_CTX, ROWS, LAT), BF16),
            pltpu.VMEM((PAIRS, 2, LAT), BF16),
            pltpu.VMEM((N_EXP, 2, LAT), BF16),
            pltpu.VMEM((N_EXP, 2, KVL + 128), BF16),
            pltpu.VMEM((N_EXP, 2, KVL + 128), BF16),
            pltpu.VMEM((N_CTX // 2, 2 * SLOTS, VD), BF16),
            pltpu.VMEM((N_CTX * N_X, 2 * SLOTS, VD), BF16),
            pltpu.VMEM((N_X, VD, COLS), BF16),
            pltpu.VMEM((N_Z, 8, COLS), BF16),
            pltpu.VMEM((2, 4, 8, COLS), BF16),
            pltpu.VMEM((2, 8, COLS), BF16),
            pltpu.VMEM((9, 8, COLS), BF16),
            pltpu.VMEM((8, 1, COLS), F32),
            pltpu.VMEM((8, 1, COLS), F32),
            pltpu.VMEM((TOPK, ROWS), jnp.int32),
            pltpu.VMEM((2, ROWS, ROWS), BF16),
            pltpu.VMEM((N_Z, 2, N_X, COLS), BF16),
            pltpu.VMEM((8, 1, COLS), F32),
            pltpu.VMEM((8, 1, COLS), F32),
            pltpu.VMEM((2, N_X, 16, COLS), BF16),
            pltpu.VMEM((8, 16, COLS), BF16),
            pltpu.SemaphoreType.DMA((6,)),
            pltpu.SemaphoreType.DMA((3,)),
            pltpu.SemaphoreType.DMA((14,)),
            pltpu.SemaphoreType.DMA((14,)),
            pltpu.SemaphoreType.DMA((5,)),
        ],
        compiler_params=pltpu.CompilerParams(
            collective_id=0, has_side_effects=True, vmem_limit_bytes=60 * 1024 * 1024
        ),
        cost_estimate=pl.CostEstimate(
            flops=600_000_000, bytes_accessed=8_000_000, transcendentals=40_000
        ),
    )(
        owner_slot,
        cached_len,
        owner_slot.reshape(1, N_CTX * ROWS),
        cached_len.reshape(1, N_CTX * ROWS),
        jnp.asarray(half).reshape(1, RD // 2),
        expert_ids.T,
        residual,
        ffn_gain.reshape(1, D),
        prefill_cache,
        query_latent,
        new_latent,
        wq_up.reshape(QL, QW).T,
        wk_up.reshape(NOPE, KVL),
        wv_up.reshape(KVL, VD),
        w_out,
    )
    return pl.pallas_call(
        place_results,
        out_shape=(
            jax.ShapeDtypeStruct((1, D), BF16),
            jax.ShapeDtypeStruct((1, 4, CAP, D), BF16),
        ),
        in_specs=[vmem] * 2,
        out_specs=(vmem, vmem),
    )(hidden, expert_in)


def solution(mesh):
    placed = (
        P("ctx", "exp", None),
        P(),
        P(),
        P("ctx", None),
        P("ctx", None),
        P(None, "exp", None),
        P("exp", None, None),
        P("exp", None, None),
        P("exp", None),
        P(("ctx", "exp"), None),
        P(),
        P("ctx", None),
    )
    return jax.shard_map(
        on_device,
        mesh=mesh,
        in_specs=placed,
        out_specs=(P(("ctx", "exp"), None), P("ctx", "exp", None, None)),
        check_vma=False,
    )
```

```python
import math

import jax
import jax.numpy as jnp
import numpy as np
from jax import lax
from jax.experimental import pallas as pl
from jax.experimental.pallas import tpu as pltpu
from jax.sharding import PartitionSpec as P

MESH = pl.DeviceIdType.MESH
F32 = jnp.float32
BF16 = jnp.bfloat16
N_CTX, N_EXP, N_X, N_Z = 8, 64, 4, 16
ROWS, LLOC, LAT, KVL, NOPE, RD, VD = 64, 8, 576, 512, 128, 64, 128
QL, D, CAP, TOPK, SLOTS = 1536, 7168, 4, 8, 16
QW = NOPE + RD
COLS = D // 8
PAIRS, NEAR = ROWS // 2, N_Z // 2
SCALE = 1.0 / math.sqrt(QW)


def dot(a, b, ca=1, cb=0):
    return lax.dot_general(a, b, (((ca,), (cb,)), ((), ())), preferred_element_type=F32)


def send(src, dst, send_sem, recv_sem, device):
    pltpu.make_async_remote_copy(
        src_ref=src,
        dst_ref=dst,
        send_sem=send_sem,
        recv_sem=recv_sem,
        device_id=device,
        device_id_type=MESH,
    ).start()


def drain(ref, sem):
    pltpu.make_async_copy(ref, ref, sem).wait()


def each(low, high, body):
    def step(k, carry):
        body(k)
        return carry

    lax.fori_loop(low, high, step, 0)


def offset(i, size):
    far = size // 2 - i // 2
    return jnp.where(i % 2 == 0, far, size - far)


def split(value):
    high = value.astype(BF16).astype(F32)
    middle = (value - high).astype(BF16).astype(F32)
    return high, middle, value - high - middle


def one_hot(mask):
    return mask.astype(F32).astype(BF16)


def own_part(row, y, core):
    part = row[:, 0:128]
    for i in range(1, N_CTX // 2):
        part = jnp.where(y == i, row[:, i * 128 : (i + 1) * 128], part)
    return jnp.where(core == 0, part[:, :ROWS], part[:, ROWS:])


def kernel(
    lens_s,
    owner_row,
    lens_row,
    freqs,
    ids,
    residual,
    gain,
    cache_hbm,
    ql_hbm,
    nl_hbm,
    wq_hbm,
    wk_hbm,
    wv_hbm,
    wo_hbm,
    hidden_ref,
    expert_ref,
    ql,
    wq,
    wk,
    wv,
    stage,
    ropes,
    kbuf,
    rbuf,
    nl,
    qout,
    qgot,
    nlout,
    nlgot,
    qsend,
    qrecv,
    lsend,
    lrecv,
    hsend,
    hall,
    wbuf,
    psend,
    passed,
    psum,
    precv,
    rsend,
    resid,
    other_ids,
    selection,
    zbuf,
    osend,
    orecv,
    slots,
    gbuf,
    load_sem,
    own_sem,
    send_sem,
    recv_sem,
    z_sem,
):
    c = lax.axis_index("ctx")
    e = lax.axis_index("exp")
    y, core = c // 2, lax.rem(c, 2)
    z, x = e // N_X, lax.rem(e, N_X)

    loads = [
        pltpu.make_async_copy(src, dst, load_sem.at[i])
        for i, (src, dst) in enumerate(
            [
                (ql_hbm, ql),
                (wq_hbm, wq),
                (wk_hbm, wk),
                (wv_hbm, wv),
                (nl_hbm, nl),
                (cache_hbm.at[:, :, pl.ds(KVL, RD)], stage),
            ]
        )
    ]
    for load in loads:
        load.start()

    square_row = lax.broadcasted_iota(jnp.int32, (ROWS, ROWS), 0)
    square_column = lax.broadcasted_iota(jnp.int32, (ROWS, ROWS), 1)
    eye, earlier = square_row == square_column, square_row < square_column
    slot_line = lax.broadcasted_iota(jnp.int32, (N_CTX * SLOTS, ROWS), 0)

    def upright(row):
        return jnp.sum(jnp.where(eye, row, 0.0), 1, keepdims=True)

    def count(mask):
        return jnp.sum(jnp.where(mask, 1.0, 0.0), 0, keepdims=True)

    def slots_of(part, rank):
        return one_hot(slot_line == (part * SLOTS + rank).astype(jnp.int32))

    request = lax.broadcasted_iota(jnp.int32, (ROWS, N_CTX * ROWS), 1)
    held = owner_row[...] == c * ROWS + lax.broadcasted_iota(jnp.int32, request.shape, 0)
    shard = jnp.sum(jnp.where(held, (request // ROWS).astype(F32), 0.0), 1, keepdims=True)
    shard_row = jnp.sum(jnp.where(eye, shard, 0.0), 0, keepdims=True)
    outbound = slots_of(shard_row, count((shard == shard_row) & earlier))
    mine = own_part(owner_row[...], y, core)
    owner, target = (mine // ROWS).astype(F32), mine.astype(F32)
    lower = (upright(owner) == owner) & (upright(target) < target)
    inbound = slots_of(owner, count(lower))

    barrier = pltpu.get_barrier_semaphore()
    sent, due = [], {}

    def track(name, ref, i):
        sent.append((ref, send_sem.at[i]))
        due[name] = (ref, recv_sem.at[i])

    def arrive(name):
        drain(*due.pop(name))

    def greet(device):
        pl.semaphore_signal(barrier, inc=1, device_id=device, device_id_type=MESH)

    each(1, N_EXP, lambda k: greet((c, lax.rem(e + k, N_EXP))))

    def greet_plane(k):
        for i in range(N_X):
            greet((lax.rem(c + k, N_CTX), z * N_X + i))

    each(1, N_CTX, greet_plane)

    loads[0].wait()
    loads[1].wait()
    q = dot(ql[...], wq[...], 1, 1).astype(BF16)
    qout[...] = dot(outbound, q).astype(BF16).reshape(N_CTX, SLOTS, QW)
    qgot[c] = qout[c]
    loads[4].wait()
    loads[5].wait()
    parts = stage[...].astype(F32).reshape(PAIRS, 2, LLOC, RD)
    ropes[...] = jnp.concatenate([parts[:, 0], parts[:, 1]], 2).astype(BF16)

    pl.semaphore_wait(barrier, N_EXP - 1 + (N_CTX - 1) * N_X)

    def send_q(k):
        to = lax.rem(c + offset(k, N_CTX), N_CTX)
        send(qout.at[to], qgot.at[c], send_sem.at[0], recv_sem.at[0], (to, e))

    each(1, N_CTX, send_q)
    track("q", qgot.at[pl.ds(0, N_CTX - 1)], 0)

    pair = lax.rem(e, PAIRS)
    def latents(first):
        return cache_hbm.at[pl.ds(2 * first, 2), :, pl.ds(0, KVL)]

    home = NEAR // 2 * N_X + x
    own = [
        pltpu.make_async_copy(latents(pair), kbuf.at[home], recv_sem.at[1]),
        pltpu.make_async_copy(ropes.at[pair], rbuf.at[home], recv_sem.at[13]),
    ]
    for copy in own:
        copy.start()

    def send_cache(i):
        step = i // N_X
        near = NEAR // 2 - (step + 1) // 2
        away = jnp.where(step % 2 == 1, near, N_Z - near)
        away = jnp.where((step == 0) & (z % 2 == 0), NEAR // 2, away)
        to_z = lax.rem(z + away, N_Z)
        to_x = lax.rem(x + i + jnp.where(step == NEAR - 1, 1, 0), N_X)
        into = lax.rem(N_Z - away + NEAR // 2, NEAR) * N_X + x
        first = lax.rem(to_z, NEAR) * N_X + to_x
        to = (c, to_z * N_X + to_x)
        send(latents(first), kbuf.at[into], send_sem.at[1], recv_sem.at[1], to)
        send(ropes.at[first], rbuf.at[into], send_sem.at[13], recv_sem.at[13], to)

    each(0, PAIRS - 1, send_cache)
    sent.append((kbuf.at[pl.ds(0, PAIRS - 1)], send_sem.at[1]))
    due["cache"] = (kbuf, recv_sem.at[1])
    sent.append((rbuf.at[pl.ds(0, PAIRS - 1)], send_sem.at[13]))
    due["ropes"] = (rbuf, recv_sem.at[13])


    nlout[...] = dot(outbound, nl[...]).astype(BF16).reshape(N_CTX, SLOTS, LAT)
    nlgot[c] = nlout[c]

    def send_new(k):
        to = lax.rem(c + offset(k, N_CTX), N_CTX)
        send(nlout.at[to], nlgot.at[c], send_sem.at[2], recv_sem.at[2], (to, e))

    each(1, N_CTX, send_new)
    track("new", nlgot.at[pl.ds(0, N_CTX - 1)], 2)

    mine_row, block = core * N_X + x, x * 2 + core
    for i in range(8):
        rsend[i] = residual[:, i * COLS : (i + 1) * COLS].astype(F32)
    resid[mine_row] = rsend[block]

    def send_residual(k):
        to_x, to_core = lax.rem(x + k // 2, N_X), lax.rem(core + k, 2)
        to = (y * 2 + to_core, z * N_X + to_x)
        send(rsend.at[to_x * 2 + to_core], resid.at[mine_row], send_sem.at[8], recv_sem.at[8], to)

    each(1, 8, send_residual)
    track("residual", resid.at[pl.ds(0, 7)], 8)

    send(ids, other_ids, send_sem.at[11], recv_sem.at[11], (y * 2 + 1 - core, e))
    track("ids", other_ids, 11)

    lengths = own_part(lens_row[...], y, core).astype(F32)
    angles = upright(lengths) * freqs[...]
    cosines, sines = jnp.cos(angles), jnp.sin(angles)
    loads[2].wait()
    arrive("q")
    q = dot(inbound, qgot[...].reshape(N_CTX * SLOTS, QW), 0, 0)
    absorbed = dot(q[:, :NOPE].astype(BF16), wk[...])
    first, second = q[:, NOPE : NOPE + RD // 2], q[:, NOPE + RD // 2 :]
    turned = jnp.concatenate(
        [first * cosines - second * sines, first * sines + second * cosines], 1
    )
    absorbed = jnp.concatenate([absorbed, turned], 1).astype(BF16)
    qsend[...] = absorbed.reshape(PAIRS, 2, LAT)
    own_query = pltpu.make_async_copy(qsend.at[pair], qrecv.at[e], own_sem.at[1])
    own_query.start()
    due["own_query"] = (qrecv.at[e], own_sem.at[1])

    def send_query(k):
        j = lax.rem(e + offset(k, N_EXP), N_EXP)
        send(qsend.at[lax.rem(j, PAIRS)], qrecv.at[e], send_sem.at[4], recv_sem.at[4], (c, j))

    each(1, N_EXP, send_query)
    track("query", qrecv.at[pl.ds(0, N_EXP - 1)], 4)


    def columns(i):
        return wo_hbm.at[:, pl.ds(pl.multiple_of((i * 2 + core) * COLS, 128), COLS)]

    own_w = pltpu.make_async_copy(columns(x), wbuf.at[x], own_sem.at[0])
    own_w.start()
    due["own_w"] = (wbuf.at[x], own_sem.at[0])

    def send_w(k):
        i = lax.rem(x + k, N_X)
        send(columns(i), wbuf.at[x], send_sem.at[3], recv_sem.at[3], (c, z * N_X + i))

    each(1, N_X, send_w)
    track("w", wbuf.at[pl.ds(0, N_X - 1)], 3)

    arrive("ids")
    turn = lax.broadcasted_iota(jnp.int32, (1, ROWS), 1) // N_X
    turn = jnp.where(turn == 0, z, z + N_Z - offset(turn, N_Z)) % N_Z
    held = turn * N_X + lax.broadcasted_iota(jnp.int32, (1, ROWS), 1) % N_X
    held = one_hot(lax.broadcasted_iota(jnp.int32, (ROWS, ROWS), 0) == held)
    expert = z * 16 + lax.broadcasted_iota(jnp.int32, (16, ROWS), 0)
    line = lax.broadcasted_iota(jnp.int32, (ROWS, 16), 0)
    widen = one_hot(line // CAP == lax.broadcasted_iota(jnp.int32, (ROWS, 16), 1))
    slot_of = (lax.broadcasted_iota(jnp.int32, (ROWS, ROWS), 0) % CAP).astype(F32)
    for g in range(2):
        names = jnp.where(core == g, ids[...], other_ids[...])
        named = jnp.zeros((16, ROWS), F32)
        for i in range(TOPK):
            named = named + (names[i : i + 1] == expert).astype(F32)
        named = named.astype(BF16)
        before = dot(named, one_hot(earlier)).astype(BF16)
        taken = (dot(widen, named) > 0.5) & (dot(widen, before) == slot_of)
        selection[g] = dot(one_hot(taken), held).astype(BF16)

    first_request = c * ROWS + 2 * pair
    width = PAIRS * LLOC
    slot = lax.broadcasted_iota(jnp.int32, (1, width), 1) // LLOC
    from_z = z + slot // N_X + N_Z - NEAR // 2
    from_z = jnp.where((slot < N_X) & (z % 2 == 1), z + NEAR // 2, from_z) % N_Z
    position = (from_z * N_X + slot % N_X) * LLOC
    position = position + lax.broadcasted_iota(jnp.int32, (1, width), 1) % LLOC
    even = lax.broadcasted_iota(jnp.int32, (2 * N_EXP, 1), 0) % 2 == 0
    valid = position < jnp.where(even, lens_s[first_request], lens_s[first_request + 1])
    wanted = 2 * pair + jnp.minimum(lax.broadcasted_iota(jnp.int32, (16, ROWS), 0), 1)
    pick = one_hot(lax.broadcasted_iota(jnp.int32, (16, ROWS), 1) == wanted)
    pick = dot(pick, inbound, 1, 1).astype(BF16)
    arrive("new")
    new = dot(pick, nlgot[...].reshape(N_CTX * SLOTS, LAT))
    arrive("cache")
    arrive("ropes")
    keys = [kbuf[:, t].astype(F32).reshape(width, KVL).astype(BF16) for t in range(2)]
    turned_keys = rbuf[...].astype(F32).reshape(width, 2 * RD).astype(BF16)
    half = lax.broadcasted_iota(jnp.int32, (2 * N_EXP, 2 * RD), 1) < RD
    arrive("own_query")
    arrive("query")
    queries = qrecv[...].reshape(2 * N_EXP, LAT)
    new_scores = dot(queries, new.astype(BF16), 1, 1) * SCALE
    new_scores = jnp.where(even, new_scores[:, 0:1], new_scores[:, 1:2])
    new_scores = jnp.where(e < PAIRS, new_scores, -1e30)
    latent_part = queries[:, :KVL]
    turned_part = queries[:, KVL:].astype(F32)
    turned_part = jnp.concatenate([turned_part, turned_part], 1)
    turned_part = jnp.where(half == even, turned_part, 0.0).astype(BF16)
    scores = jnp.where(even, dot(latent_part, keys[0], 1, 1), dot(latent_part, keys[1], 1, 1))
    scores = (scores + dot(turned_part, turned_keys, 1, 1)) * SCALE
    top = jnp.max(jnp.where(valid, scores, -1e30), 1, keepdims=True)
    top = jnp.maximum(top, new_scores)
    weights = jnp.where(valid, jnp.exp(scores - top), 0.0)
    new_weight = jnp.where(e < PAIRS, jnp.exp(new_scores - top), 0.0)
    total = jnp.sum(weights, 1, keepdims=True) + new_weight
    mixed = dot(jnp.where(even, weights, 0.0).astype(BF16), keys[0])
    mixed = mixed + dot(jnp.where(even, 0.0, weights).astype(BF16), keys[1])
    mixed = mixed + new_weight.astype(BF16).astype(F32) * jnp.where(
        even, new[0:1, :KVL], new[1:2, :KVL]
    )
    some = total > 0.0
    divisor = jnp.where(some, total, 1.0)
    parts = split(jnp.where(some, top + jnp.log(divisor), -1e30))
    lane = lax.broadcasted_iota(jnp.int32, (2 * N_EXP, 128), 1)
    tail = jnp.zeros((2 * N_EXP, 128), F32)
    for i in range(3):
        tail = jnp.where(lane == i, parts[i], tail)
    latent = jnp.concatenate([mixed / divisor, tail], 1).astype(BF16)
    lsend[...] = latent.reshape(N_EXP, 2, KVL + 128)
    own_latent = pltpu.make_async_copy(lsend.at[e], lrecv.at[e], own_sem.at[2])
    own_latent.start()
    due["own_latent"] = (lrecv.at[e], own_sem.at[2])

    def send_latent(k):
        j = lax.rem(e + offset(k, N_EXP), N_EXP)
        send(lsend.at[j], lrecv.at[e], send_sem.at[5], recv_sem.at[5], (c, j))

    each(1, N_EXP, send_latent)
    track("latent", lrecv.at[pl.ds(0, N_EXP - 1)], 5)

    def ranks(owner):
        return count((upright(owner) == owner) & earlier)

    bucket = slots_of(owner, ranks(owner))
    keys = []
    for i in range(N_CTX):
        owner = owner_row[:, i * ROWS : (i + 1) * ROWS] // ROWS
        key = (i * 2 + owner - 2 * y) * SLOTS + ranks(owner.astype(F32)).astype(jnp.int32)
        keys.append(jnp.where(owner // 2 == y, key, -1))
    keys = jnp.concatenate(keys, 1)
    keys = one_hot(lax.broadcasted_iota(jnp.int32, (N_CTX * 2 * SLOTS, N_CTX * ROWS), 0) == keys)
    order = lax.broadcasted_iota(jnp.int32, (2 * ROWS, N_CTX * ROWS), 0)
    rest = order % 8
    wanted = (y * 2 + rest // N_X) * ROWS + (order // 8) * N_X + rest % N_X
    place = dot(one_hot(owner_row[...] == wanted), keys, 1, 1).astype(BF16)

    loads[3].wait()
    arrive("own_latent")
    arrive("latent")
    at = c * N_X + x
    halves = lrecv[...].reshape(2 * N_EXP, KVL + 128).astype(F32)
    sums = halves[:, KVL : KVL + 1] + halves[:, KVL + 1 : KVL + 2] + halves[:, KVL + 2 : KVL + 3]
    peak = jnp.maximum(sums[:ROWS], sums[ROWS:])
    low, high = jnp.exp(sums[:ROWS] - peak), jnp.exp(sums[ROWS:] - peak)
    latent = (low * halves[:ROWS, :KVL] + high * halves[ROWS:, :KVL]) / (low + high)
    value = dot(latent.astype(BF16), wv[...]).astype(BF16)
    hsend[...] = dot(bucket, value).astype(BF16).reshape(N_CTX // 2, 2 * SLOTS, VD)
    hall[at] = hsend[y]

    def send_heads(k):
        to_c = lax.rem(c + offset(k, N_CTX), N_CTX)
        for i in range(N_X):
            to = (to_c, z * N_X + lax.rem(x + i, N_X))
            send(hsend.at[to_c // 2], hall.at[at], send_sem.at[6], recv_sem.at[6], to)

    def send_heads_x(k):
        to = (c, z * N_X + lax.rem(x + k, N_X))
        send(hsend.at[y], hall.at[at], send_sem.at[6], recv_sem.at[6], to)

    each(1, N_CTX, send_heads)
    each(1, N_X, send_heads_x)
    track("heads", hall.at[pl.ds(0, N_CTX * N_X - 1)], 6)

    arrive("own_w")
    arrive("w")
    arrive("heads")
    partial = jnp.zeros((2 * ROWS, COLS), F32)
    heads = hall[...].reshape(N_CTX, N_X, 2 * SLOTS, VD)
    for i in range(N_X):
        head = dot(place, heads[:, i].reshape(N_CTX * 2 * SLOTS, VD)).astype(BF16)
        partial = partial + dot(head, wbuf[i])
    psend[...] = partial.reshape(N_Z, 8, COLS).astype(BF16)
    precv[4] = psend[z]

    def at_z(hop):
        return lax.rem(z + hop + N_Z, N_Z)

    def along_z(source, into, hop, recv):
        send(source, into, send_sem.at[7], recv, (c, at_z(hop) * N_X + x))

    for j in range(3):
        along_z(psend.at[at_z(-5 - j)], passed.at[0, j], -1 - j, z_sem.at[0])
        along_z(psend.at[at_z(5 + j)], passed.at[1, j], 1 + j, z_sem.at[1])

    @pl.when(z % 2 == 0)
    def _():
        along_z(psend.at[at_z(8)], passed.at[0, 3], -4, z_sem.at[2])

    @pl.when(z % 2 == 1)
    def _():
        along_z(psend.at[at_z(8)], passed.at[1, 3], 4, z_sem.at[2])

    for j in range(1, 4):
        along_z(psend.at[at_z(j)], precv.at[4 - j], j, recv_sem.at[7])
        along_z(psend.at[at_z(-j)], precv.at[4 + j], -j, recv_sem.at[7])
    for side in range(2):
        drain(passed.at[side, pl.ds(0, 3)], z_sem.at[side])
        hop = -4 if side == 0 else 4
        through = psend[at_z(hop)].astype(F32)
        for j in range(3):
            through = through + passed[side, j].astype(F32)
        psum[side] = through.astype(BF16)

        @pl.when(z % 2 == side)
        def _():
            drain(passed.at[side, 3], z_sem.at[2])
            psum[side] = (through + passed[side, 3].astype(F32)).astype(BF16)

        along_z(psum.at[side], precv.at[4 - hop], hop, recv_sem.at[7])
    sent.append((psend.at[pl.ds(0, N_Z - 1)], send_sem.at[7]))
    due["partial"] = (precv.at[pl.ds(0, 8)], recv_sem.at[7])
    arrive("partial")
    summed = precv[0].astype(F32)
    for i in range(1, 9):
        summed = summed + precv[i].astype(F32)

    arrive("residual")
    hidden = summed + resid[:, 0, :]
    zbuf[0] = hidden.astype(BF16).reshape(2, N_X, COLS)

    def pass_on(source, into, hop, recv):
        send(zbuf.at[source], zbuf.at[into], send_sem.at[9], recv, (c, at_z(hop) * N_X + x))

    pass_on(0, 8, 4, z_sem.at[3])
    pass_on(0, 9, -4, z_sem.at[4])
    for j in range(1, 4):
        pass_on(0, 16 - 2 * j, j, recv_sem.at[9])
        pass_on(0, 17 - 2 * j, -j, recv_sem.at[9])

    osend[:, 0, :] = hidden
    orecv[block] = osend[mine_row]

    def send_row(k):
        to_x, to_core = lax.rem(x + k // 2, N_X), lax.rem(core + k, 2)
        to = (y * 2 + to_core, z * N_X + to_x)
        send(osend.at[to_core * N_X + to_x], orecv.at[block], send_sem.at[12], recv_sem.at[12], to)

    each(1, 8, send_row)
    track("row", orecv.at[pl.ds(0, 7)], 12)

    for side in range(2):
        drain(zbuf.at[8 + side], z_sem.at[3 + side])
        way = 1 - 2 * side

        @pl.when(z % 2 == side)
        def _():
            pass_on(8 + side, 1, 4 * way, recv_sem.at[9])

        for j in range(3):
            pass_on(8 + side, 2 + 2 * j + side, (3 - j) * way, recv_sem.at[9])
    sent.append((zbuf.at[pl.ds(0, N_Z - 1)], send_sem.at[9]))
    due["columns"] = (zbuf.at[pl.ds(0, N_Z - 3)], recv_sem.at[9])

    arrive("columns")
    for g in range(2):
        rows = dot(selection[g], zbuf[:, g].reshape(ROWS, COLS)).astype(BF16)
        slots[g] = rows.reshape(N_X, 16, COLS)
        for i in range(1, N_X):
            to_x = lax.rem(x + i, N_X)
            to = (y * 2 + g, z * N_X + to_x)
            send(slots.at[g, to_x], gbuf.at[block], send_sem.at[10], recv_sem.at[10], to)
    to = (y * 2 + 1 - core, e)
    send(slots.at[1 - core, x], gbuf.at[block], send_sem.at[10], recv_sem.at[10], to)
    track("slots", gbuf.at[pl.ds(0, 7)], 10)
    gbuf[block] = slots[core, x]
    arrive("row")
    for i in range(8):
        hidden_ref[:, i * COLS : (i + 1) * COLS] = orecv[i].astype(BF16)
    arrive("slots")

    square = jnp.zeros((16, 1), F32)
    for i in range(8):
        rows = gbuf[i].astype(F32)
        square = square + jnp.sum(rows * rows, 1, keepdims=True)
    factor = lax.rsqrt(square * (1.0 / D) + 1e-06)
    for i in range(8):
        there = slice(i * COLS, (i + 1) * COLS)
        expert_ref[:, there] = (gbuf[i].astype(F32) * factor * gain[:, there]).astype(BF16)

    for ref, sem in sent:
        drain(ref, sem)


def place_results(hidden, expert_in, hidden_ref, expert_ref):
    hidden_ref[...] = hidden[...]
    for i in range(4):
        expert_ref[0, i] = expert_in[i * CAP : (i + 1) * CAP]


def on_device(
    prefill_cache,
    owner_slot,
    cached_len,
    query_latent,
    new_latent,
    wq_up,
    wk_up,
    wv_up,
    w_out,
    residual,
    ffn_gain,
    expert_ids,
):
    half = (10000.0 ** (-2.0 * np.arange(RD // 2, dtype=np.float32) / RD)).astype(np.float32)
    smem = pl.BlockSpec(memory_space=pltpu.SMEM)
    vmem = pl.BlockSpec(memory_space=pltpu.VMEM)
    anywhere = pl.BlockSpec(memory_space=pl.ANY)
    hidden, expert_in = pl.pallas_call(
        kernel,
        out_shape=(
            jax.ShapeDtypeStruct((1, D), BF16),
            jax.ShapeDtypeStruct((4 * CAP, D), BF16),
        ),
        in_specs=[smem] + [vmem] * 6 + [anywhere] * 7,
        out_specs=(vmem, vmem),
        scratch_shapes=[
            pltpu.VMEM((ROWS, QL), BF16),
            pltpu.VMEM((QW, QL), BF16),
            pltpu.VMEM((NOPE, KVL), BF16),
            pltpu.VMEM((KVL, VD), BF16),
            pltpu.VMEM((N_EXP, LLOC, RD), BF16),
            pltpu.VMEM((PAIRS, LLOC, 2 * RD), BF16),
            pltpu.VMEM((PAIRS, 2, LLOC, KVL), BF16),
            pltpu.VMEM((PAIRS, LLOC, 2 * RD), BF16),
            pltpu.VMEM((ROWS, LAT), BF16),
            pltpu.VMEM((N_CTX, SLOTS, QW), BF16),
            pltpu.VMEM((N_CTX, SLOTS, QW), BF16),
            pltpu.VMEM((N_CTX, SLOTS, LAT), BF16),
            pltpu.VMEM((N_CTX, SLOTS, LAT), BF16),
            pltpu.VMEM((PAIRS, 2, LAT), BF16),
            pltpu.VMEM((N_EXP, 2, LAT), BF16),
            pltpu.VMEM((N_EXP, 2, KVL + 128), BF16),
            pltpu.VMEM((N_EXP, 2, KVL + 128), BF16),
            pltpu.VMEM((N_CTX // 2, 2 * SLOTS, VD), BF16),
            pltpu.VMEM((N_CTX * N_X, 2 * SLOTS, VD), BF16),
            pltpu.VMEM((N_X, VD, COLS), BF16),
            pltpu.VMEM((N_Z, 8, COLS), BF16),
            pltpu.VMEM((2, 4, 8, COLS), BF16),
            pltpu.VMEM((2, 8, COLS), BF16),
            pltpu.VMEM((9, 8, COLS), BF16),
            pltpu.VMEM((8, 1, COLS), F32),
            pltpu.VMEM((8, 1, COLS), F32),
            pltpu.VMEM((TOPK, ROWS), jnp.int32),
            pltpu.VMEM((2, ROWS, ROWS), BF16),
            pltpu.VMEM((N_Z, 2, N_X, COLS), BF16),
            pltpu.VMEM((8, 1, COLS), F32),
            pltpu.VMEM((8, 1, COLS), F32),
            pltpu.VMEM((2, N_X, 16, COLS), BF16),
            pltpu.VMEM((8, 16, COLS), BF16),
            pltpu.SemaphoreType.DMA((6,)),
            pltpu.SemaphoreType.DMA((3,)),
            pltpu.SemaphoreType.DMA((14,)),
            pltpu.SemaphoreType.DMA((14,)),
            pltpu.SemaphoreType.DMA((5,)),
        ],
        compiler_params=pltpu.CompilerParams(
            collective_id=0, has_side_effects=True, vmem_limit_bytes=60 * 1024 * 1024
        ),
        cost_estimate=pl.CostEstimate(
            flops=600_000_000, bytes_accessed=8_000_000, transcendentals=40_000
        ),
    )(
        cached_len,
        owner_slot.reshape(1, N_CTX * ROWS),
        cached_len.reshape(1, N_CTX * ROWS),
        jnp.asarray(half).reshape(1, RD // 2),
        expert_ids.T,
        residual,
        ffn_gain.reshape(1, D),
        prefill_cache,
        query_latent,
        new_latent,
        wq_up.reshape(QL, QW).T,
        wk_up.reshape(NOPE, KVL),
        wv_up.reshape(KVL, VD),
        w_out,
    )
    return pl.pallas_call(
        place_results,
        out_shape=(
            jax.ShapeDtypeStruct((1, D), BF16),
            jax.ShapeDtypeStruct((1, 4, CAP, D), BF16),
        ),
        in_specs=[vmem] * 2,
        out_specs=(vmem, vmem),
    )(hidden, expert_in)


def solution(mesh):
    placed = (
        P("ctx", "exp", None),
        P(),
        P(),
        P("ctx", None),
        P("ctx", None),
        P(None, "exp", None),
        P("exp", None, None),
        P("exp", None, None),
        P("exp", None),
        P(("ctx", "exp"), None),
        P(),
        P("ctx", None),
    )
    return jax.shard_map(
        on_device,
        mesh=mesh,
        in_specs=placed,
        out_specs=(P(("ctx", "exp"), None), P("ctx", "exp", None, None)),
        check_vma=False,
    )
```

```python
import math

import jax
import jax.numpy as jnp
import numpy as np
from jax import lax
from jax.experimental import pallas as pl
from jax.experimental.pallas import tpu as pltpu
from jax.sharding import PartitionSpec as P

MESH = pl.DeviceIdType.MESH
F32 = jnp.float32
BF16 = jnp.bfloat16
N_CTX, N_EXP, N_X, N_Z = 8, 64, 4, 16
ROWS, LLOC, LAT, KVL, NOPE, RD, VD = 64, 8, 576, 512, 128, 64, 128
QL, D, CAP, TOPK, SLOTS = 1536, 7168, 4, 8, 16
QW = NOPE + RD
COLS = D // 8
PAIRS, NEAR = ROWS // 2, N_Z // 2
SCALE = 1.0 / math.sqrt(QW)


def dot(a, b, ca=1, cb=0):
    return lax.dot_general(a, b, (((ca,), (cb,)), ((), ())), preferred_element_type=F32)


def send(src, dst, send_sem, recv_sem, device):
    pltpu.make_async_remote_copy(
        src_ref=src,
        dst_ref=dst,
        send_sem=send_sem,
        recv_sem=recv_sem,
        device_id=device,
        device_id_type=MESH,
    ).start()


def drain(ref, sem):
    pltpu.make_async_copy(ref, ref, sem).wait()


def each(low, high, body):
    def step(k, carry):
        body(k)
        return carry

    lax.fori_loop(low, high, step, 0)


def offset(i, size):
    far = size // 2 - i // 2
    return jnp.where(i % 2 == 0, far, size - far)


def split(value):
    high = value.astype(BF16).astype(F32)
    middle = (value - high).astype(BF16).astype(F32)
    return high, middle, value - high - middle


def one_hot(mask):
    return mask.astype(F32).astype(BF16)


def own_part(row, y, core):
    part = row[:, 0:128]
    for i in range(1, N_CTX // 2):
        part = jnp.where(y == i, row[:, i * 128 : (i + 1) * 128], part)
    return jnp.where(core == 0, part[:, :ROWS], part[:, ROWS:])


def kernel(
    lens_s,
    owner_row,
    lens_row,
    freqs,
    ids,
    residual,
    gain,
    cache_hbm,
    ql_hbm,
    nl_hbm,
    wq_hbm,
    wk_hbm,
    wv_hbm,
    wo_hbm,
    hidden_ref,
    expert_ref,
    ql,
    wq,
    wk,
    wv,
    stage,
    ropes,
    kbuf,
    rbuf,
    nl,
    qout,
    qgot,
    nlout,
    nlgot,
    qsend,
    qrecv,
    lsend,
    lrecv,
    hsend,
    hall,
    wbuf,
    psend,
    passed,
    psum,
    precv,
    rsend,
    resid,
    other_ids,
    selection,
    zbuf,
    osend,
    orecv,
    slots,
    gbuf,
    load_sem,
    own_sem,
    send_sem,
    recv_sem,
    z_sem,
):
    c = lax.axis_index("ctx")
    e = lax.axis_index("exp")
    y, core = c // 2, lax.rem(c, 2)
    z, x = e // N_X, lax.rem(e, N_X)

    loads = [
        pltpu.make_async_copy(src, dst, load_sem.at[i])
        for i, (src, dst) in enumerate(
            [
                (ql_hbm, ql),
                (wq_hbm, wq),
                (wk_hbm, wk),
                (wv_hbm, wv),
                (nl_hbm, nl),
                (cache_hbm.at[:, :, pl.ds(KVL, RD)], stage),
            ]
        )
    ]
    for load in loads:
        load.start()

    square_row = lax.broadcasted_iota(jnp.int32, (ROWS, ROWS), 0)
    square_column = lax.broadcasted_iota(jnp.int32, (ROWS, ROWS), 1)
    eye, earlier = square_row == square_column, square_row < square_column
    slot_line = lax.broadcasted_iota(jnp.int32, (N_CTX * SLOTS, ROWS), 0)

    def upright(row):
        return jnp.sum(jnp.where(eye, row, 0.0), 1, keepdims=True)

    def count(mask):
        return jnp.sum(jnp.where(mask, 1.0, 0.0), 0, keepdims=True)

    def slots_of(part, rank):
        return one_hot(slot_line == (part * SLOTS + rank).astype(jnp.int32))

    request = lax.broadcasted_iota(jnp.int32, (ROWS, N_CTX * ROWS), 1)
    held = owner_row[...] == c * ROWS + lax.broadcasted_iota(jnp.int32, request.shape, 0)
    shard = jnp.sum(jnp.where(held, (request // ROWS).astype(F32), 0.0), 1, keepdims=True)
    shard_row = jnp.sum(jnp.where(eye, shard, 0.0), 0, keepdims=True)
    outbound = slots_of(shard_row, count((shard == shard_row) & earlier))
    mine = own_part(owner_row[...], y, core)
    owner, target = (mine // ROWS).astype(F32), mine.astype(F32)
    lower = (upright(owner) == owner) & (upright(target) < target)
    inbound = slots_of(owner, count(lower))

    barrier = pltpu.get_barrier_semaphore()
    sent, due = [], {}

    def track(name, ref, i):
        sent.append((ref, send_sem.at[i]))
        due[name] = (ref, recv_sem.at[i])

    def arrive(name):
        drain(*due.pop(name))

    def greet(device):
        pl.semaphore_signal(barrier, inc=1, device_id=device, device_id_type=MESH)

    each(1, N_EXP, lambda k: greet((c, lax.rem(e + k, N_EXP))))

    def greet_plane(k):
        for i in range(N_X):
            greet((lax.rem(c + k, N_CTX), z * N_X + i))

    each(1, N_CTX, greet_plane)

    loads[0].wait()
    loads[1].wait()
    q = dot(ql[...], wq[...], 1, 1).astype(BF16)
    qout[...] = dot(outbound, q).astype(BF16).reshape(N_CTX, SLOTS, QW)
    qgot[c] = qout[c]
    loads[4].wait()
    loads[5].wait()
    parts = stage[...].astype(F32).reshape(PAIRS, 2, LLOC, RD)
    ropes[...] = jnp.concatenate([parts[:, 0], parts[:, 1]], 2).astype(BF16)

    pl.semaphore_wait(barrier, N_EXP - 1 + (N_CTX - 1) * N_X)

    def send_q(k):
        to = lax.rem(c + offset(k, N_CTX), N_CTX)
        send(qout.at[to], qgot.at[c], send_sem.at[0], recv_sem.at[0], (to, e))

    each(1, N_CTX, send_q)
    track("q", qgot.at[pl.ds(0, N_CTX - 1)], 0)

    pair = lax.rem(e, PAIRS)
    def latents(first):
        return cache_hbm.at[pl.ds(2 * first, 2), :, pl.ds(0, KVL)]

    home = NEAR // 2 * N_X + x
    own = [
        pltpu.make_async_copy(latents(pair), kbuf.at[home], recv_sem.at[1]),
        pltpu.make_async_copy(ropes.at[pair], rbuf.at[home], recv_sem.at[13]),
    ]
    for copy in own:
        copy.start()

    def send_cache(i):
        step = i // N_X
        near = NEAR // 2 - (step + 1) // 2
        away = jnp.where(step % 2 == 1, near, N_Z - near)
        away = jnp.where((step == 0) & (z % 2 == 0), NEAR // 2, away)
        to_z = lax.rem(z + away, N_Z)
        to_x = lax.rem(x + i + jnp.where(step == NEAR - 1, 1, 0), N_X)
        into = lax.rem(N_Z - away + NEAR // 2, NEAR) * N_X + x
        first = lax.rem(to_z, NEAR) * N_X + to_x
        to = (c, to_z * N_X + to_x)
        send(latents(first), kbuf.at[into], send_sem.at[1], recv_sem.at[1], to)
        send(ropes.at[first], rbuf.at[into], send_sem.at[13], recv_sem.at[13], to)

    each(0, PAIRS - 1, send_cache)
    sent.append((kbuf.at[pl.ds(0, PAIRS - 1)], send_sem.at[1]))
    due["cache"] = (kbuf, recv_sem.at[1])
    sent.append((rbuf.at[pl.ds(0, PAIRS - 1)], send_sem.at[13]))
    due["ropes"] = (rbuf, recv_sem.at[13])


    nlout[...] = dot(outbound, nl[...]).astype(BF16).reshape(N_CTX, SLOTS, LAT)
    nlgot[c] = nlout[c]

    def send_new(k):
        to = lax.rem(c + offset(k, N_CTX), N_CTX)
        send(nlout.at[to], nlgot.at[c], send_sem.at[2], recv_sem.at[2], (to, e))

    each(1, N_CTX, send_new)
    track("new", nlgot.at[pl.ds(0, N_CTX - 1)], 2)

    mine_row, block = core * N_X + x, x * 2 + core
    for i in range(8):
        rsend[i] = residual[:, i * COLS : (i + 1) * COLS].astype(F32)
    resid[mine_row] = rsend[block]

    def send_residual(k):
        to_x, to_core = lax.rem(x + k // 2, N_X), lax.rem(core + k, 2)
        to = (y * 2 + to_core, z * N_X + to_x)
        send(rsend.at[to_x * 2 + to_core], resid.at[mine_row], send_sem.at[8], recv_sem.at[8], to)

    each(1, 8, send_residual)
    track("residual", resid.at[pl.ds(0, 7)], 8)

    send(ids, other_ids, send_sem.at[11], recv_sem.at[11], (y * 2 + 1 - core, e))
    track("ids", other_ids, 11)

    lengths = own_part(lens_row[...], y, core).astype(F32)
    angles = upright(lengths) * freqs[...]
    cosines, sines = jnp.cos(angles), jnp.sin(angles)
    loads[2].wait()
    arrive("q")
    q = dot(inbound, qgot[...].reshape(N_CTX * SLOTS, QW), 0, 0)
    absorbed = dot(q[:, :NOPE].astype(BF16), wk[...])
    first, second = q[:, NOPE : NOPE + RD // 2], q[:, NOPE + RD // 2 :]
    turned = jnp.concatenate(
        [first * cosines - second * sines, first * sines + second * cosines], 1
    )
    absorbed = jnp.concatenate([absorbed, turned], 1).astype(BF16)
    qsend[...] = absorbed.reshape(PAIRS, 2, LAT)
    own_query = pltpu.make_async_copy(qsend.at[pair], qrecv.at[e], own_sem.at[1])
    own_query.start()
    due["own_query"] = (qrecv.at[e], own_sem.at[1])

    def send_query(k):
        j = lax.rem(e + offset(k, N_EXP), N_EXP)
        send(qsend.at[lax.rem(j, PAIRS)], qrecv.at[e], send_sem.at[4], recv_sem.at[4], (c, j))

    each(1, N_EXP, send_query)
    track("query", qrecv.at[pl.ds(0, N_EXP - 1)], 4)


    def columns(i):
        return wo_hbm.at[:, pl.ds(pl.multiple_of((i * 2 + core) * COLS, 128), COLS)]

    own_w = pltpu.make_async_copy(columns(x), wbuf.at[x], own_sem.at[0])
    own_w.start()
    due["own_w"] = (wbuf.at[x], own_sem.at[0])

    def send_w(k):
        i = lax.rem(x + k, N_X)
        send(columns(i), wbuf.at[x], send_sem.at[3], recv_sem.at[3], (c, z * N_X + i))

    each(1, N_X, send_w)
    track("w", wbuf.at[pl.ds(0, N_X - 1)], 3)

    arrive("ids")
    turn = lax.broadcasted_iota(jnp.int32, (1, ROWS), 1) // N_X
    turn = jnp.where(turn == 0, z, z + N_Z - offset(turn, N_Z)) % N_Z
    held = turn * N_X + lax.broadcasted_iota(jnp.int32, (1, ROWS), 1) % N_X
    held = one_hot(lax.broadcasted_iota(jnp.int32, (ROWS, ROWS), 0) == held)
    expert = z * 16 + lax.broadcasted_iota(jnp.int32, (16, ROWS), 0)
    line = lax.broadcasted_iota(jnp.int32, (ROWS, 16), 0)
    widen = one_hot(line // CAP == lax.broadcasted_iota(jnp.int32, (ROWS, 16), 1))
    slot_of = (lax.broadcasted_iota(jnp.int32, (ROWS, ROWS), 0) % CAP).astype(F32)
    for g in range(2):
        names = jnp.where(core == g, ids[...], other_ids[...])
        named = jnp.zeros((16, ROWS), F32)
        for i in range(TOPK):
            named = named + (names[i : i + 1] == expert).astype(F32)
        named = named.astype(BF16)
        before = dot(named, one_hot(earlier)).astype(BF16)
        taken = (dot(widen, named) > 0.5) & (dot(widen, before) == slot_of)
        selection[g] = dot(one_hot(taken), held).astype(BF16)

    first_request = c * ROWS + 2 * pair
    width = PAIRS * LLOC
    slot = lax.broadcasted_iota(jnp.int32, (1, width), 1) // LLOC
    from_z = z + slot // N_X + N_Z - NEAR // 2
    from_z = jnp.where((slot < N_X) & (z % 2 == 1), z + NEAR // 2, from_z) % N_Z
    position = (from_z * N_X + slot % N_X) * LLOC
    position = position + lax.broadcasted_iota(jnp.int32, (1, width), 1) % LLOC
    even = lax.broadcasted_iota(jnp.int32, (2 * N_EXP, 1), 0) % 2 == 0
    valid = position < jnp.where(even, lens_s[first_request], lens_s[first_request + 1])
    wanted = 2 * pair + jnp.minimum(lax.broadcasted_iota(jnp.int32, (16, ROWS), 0), 1)
    pick = one_hot(lax.broadcasted_iota(jnp.int32, (16, ROWS), 1) == wanted)
    pick = dot(pick, inbound, 1, 1).astype(BF16)
    arrive("new")
    new = dot(pick, nlgot[...].reshape(N_CTX * SLOTS, LAT))
    arrive("cache")
    arrive("ropes")
    keys = [kbuf[:, t].astype(F32).reshape(width, KVL).astype(BF16) for t in range(2)]
    turned_keys = rbuf[...].astype(F32).reshape(width, 2 * RD).astype(BF16)
    half = lax.broadcasted_iota(jnp.int32, (2 * N_EXP, 2 * RD), 1) < RD
    arrive("own_query")
    arrive("query")
    queries = qrecv[...].reshape(2 * N_EXP, LAT)
    new_scores = dot(queries, new.astype(BF16), 1, 1) * SCALE
    new_scores = jnp.where(even, new_scores[:, 0:1], new_scores[:, 1:2])
    new_scores = jnp.where(e < PAIRS, new_scores, -1e30)
    latent_part = queries[:, :KVL]
    turned_part = queries[:, KVL:].astype(F32)
    turned_part = jnp.concatenate([turned_part, turned_part], 1)
    turned_part = jnp.where(half == even, turned_part, 0.0).astype(BF16)
    scores = jnp.where(even, dot(latent_part, keys[0], 1, 1), dot(latent_part, keys[1], 1, 1))
    scores = (scores + dot(turned_part, turned_keys, 1, 1)) * SCALE
    top = jnp.max(jnp.where(valid, scores, -1e30), 1, keepdims=True)
    top = jnp.maximum(top, new_scores)
    weights = jnp.where(valid, jnp.exp(scores - top), 0.0)
    new_weight = jnp.where(e < PAIRS, jnp.exp(new_scores - top), 0.0)
    total = jnp.sum(weights, 1, keepdims=True) + new_weight
    mixed = dot(jnp.where(even, weights, 0.0).astype(BF16), keys[0])
    mixed = mixed + dot(jnp.where(even, 0.0, weights).astype(BF16), keys[1])
    mixed = mixed + new_weight.astype(BF16).astype(F32) * jnp.where(
        even, new[0:1, :KVL], new[1:2, :KVL]
    )
    some = total > 0.0
    divisor = jnp.where(some, total, 1.0)
    parts = split(jnp.where(some, top + jnp.log(divisor), -1e30))
    lane = lax.broadcasted_iota(jnp.int32, (2 * N_EXP, 128), 1)
    tail = jnp.zeros((2 * N_EXP, 128), F32)
    for i in range(3):
        tail = jnp.where(lane == i, parts[i], tail)
    latent = jnp.concatenate([mixed / divisor, tail], 1).astype(BF16)
    lsend[...] = latent.reshape(N_EXP, 2, KVL + 128)
    own_latent = pltpu.make_async_copy(lsend.at[e], lrecv.at[e], own_sem.at[2])
    own_latent.start()
    due["own_latent"] = (lrecv.at[e], own_sem.at[2])

    def send_latent(k):
        j = lax.rem(e + offset(k, N_EXP), N_EXP)
        send(lsend.at[j], lrecv.at[e], send_sem.at[5], recv_sem.at[5], (c, j))

    each(1, N_EXP, send_latent)
    track("latent", lrecv.at[pl.ds(0, N_EXP - 1)], 5)

    def ranks(owner):
        return count((upright(owner) == owner) & earlier)

    bucket = slots_of(owner, ranks(owner))
    keys = []
    for i in range(N_CTX):
        owner = owner_row[:, i * ROWS : (i + 1) * ROWS] // ROWS
        key = (i * 2 + owner - 2 * y) * SLOTS + ranks(owner.astype(F32)).astype(jnp.int32)
        keys.append(jnp.where(owner // 2 == y, key, -1))
    keys = jnp.concatenate(keys, 1)
    keys = one_hot(lax.broadcasted_iota(jnp.int32, (N_CTX * 2 * SLOTS, N_CTX * ROWS), 0) == keys)
    order = lax.broadcasted_iota(jnp.int32, (2 * ROWS, N_CTX * ROWS), 0)
    rest = order % 8
    wanted = (y * 2 + rest // N_X) * ROWS + (order // 8) * N_X + rest % N_X
    place = dot(one_hot(owner_row[...] == wanted), keys, 1, 1).astype(BF16)

    loads[3].wait()
    arrive("own_latent")
    arrive("latent")
    at = c * N_X + x
    halves = lrecv[...].reshape(2 * N_EXP, KVL + 128).astype(F32)
    sums = halves[:, KVL : KVL + 1] + halves[:, KVL + 1 : KVL + 2] + halves[:, KVL + 2 : KVL + 3]
    peak = jnp.maximum(sums[:ROWS], sums[ROWS:])
    low, high = jnp.exp(sums[:ROWS] - peak), jnp.exp(sums[ROWS:] - peak)
    latent = (low * halves[:ROWS, :KVL] + high * halves[ROWS:, :KVL]) / (low + high)
    value = dot(latent.astype(BF16), wv[...]).astype(BF16)
    hsend[...] = dot(bucket, value).astype(BF16).reshape(N_CTX // 2, 2 * SLOTS, VD)
    hall[at] = hsend[y]

    def send_heads(k):
        to_c = lax.rem(c + offset(k, N_CTX), N_CTX)
        for i in range(N_X):
            to = (to_c, z * N_X + lax.rem(x + i, N_X))
            send(hsend.at[to_c // 2], hall.at[at], send_sem.at[6], recv_sem.at[6], to)

    def send_heads_x(k):
        to = (c, z * N_X + lax.rem(x + k, N_X))
        send(hsend.at[y], hall.at[at], send_sem.at[6], recv_sem.at[6], to)

    each(1, N_CTX, send_heads)
    each(1, N_X, send_heads_x)
    track("heads", hall.at[pl.ds(0, N_CTX * N_X - 1)], 6)

    arrive("own_w")
    arrive("w")
    arrive("heads")
    partial = jnp.zeros((2 * ROWS, COLS), F32)
    heads = hall[...].reshape(N_CTX, N_X, 2 * SLOTS, VD)
    for i in range(N_X):
        head = dot(place, heads[:, i].reshape(N_CTX * 2 * SLOTS, VD)).astype(BF16)
        partial = partial + dot(head, wbuf[i])
    psend[...] = partial.reshape(N_Z, 8, COLS).astype(BF16)
    precv[4] = psend[z]

    def at_z(hop):
        return lax.rem(z + hop + N_Z, N_Z)

    def along_z(source, into, hop, recv):
        send(source, into, send_sem.at[7], recv, (c, at_z(hop) * N_X + x))

    for j in range(3):
        along_z(psend.at[at_z(-5 - j)], passed.at[0, j], -1 - j, z_sem.at[0])
        along_z(psend.at[at_z(5 + j)], passed.at[1, j], 1 + j, z_sem.at[1])

    @pl.when(z % 2 == 0)
    def _():
        along_z(psend.at[at_z(8)], passed.at[0, 3], -4, z_sem.at[2])

    @pl.when(z % 2 == 1)
    def _():
        along_z(psend.at[at_z(8)], passed.at[1, 3], 4, z_sem.at[2])

    for j in range(1, 4):
        along_z(psend.at[at_z(j)], precv.at[4 - j], j, recv_sem.at[7])
        along_z(psend.at[at_z(-j)], precv.at[4 + j], -j, recv_sem.at[7])
    for side in range(2):
        drain(passed.at[side, pl.ds(0, 3)], z_sem.at[side])
        hop = -4 if side == 0 else 4
        through = psend[at_z(hop)].astype(F32)
        for j in range(3):
            through = through + passed[side, j].astype(F32)
        psum[side] = through.astype(BF16)

        @pl.when(z % 2 == side)
        def _():
            drain(passed.at[side, 3], z_sem.at[2])
            psum[side] = (through + passed[side, 3].astype(F32)).astype(BF16)

        along_z(psum.at[side], precv.at[4 - hop], hop, recv_sem.at[7])
    sent.append((psend.at[pl.ds(0, N_Z - 1)], send_sem.at[7]))
    due["partial"] = (precv.at[pl.ds(0, 8)], recv_sem.at[7])
    arrive("partial")
    summed = precv[0].astype(F32)
    for i in range(1, 9):
        summed = summed + precv[i].astype(F32)

    arrive("residual")
    hidden = summed + resid[:, 0, :]
    zbuf[0] = hidden.astype(BF16).reshape(2, N_X, COLS)

    def pass_on(source, into, hop, recv):
        send(zbuf.at[source], zbuf.at[into], send_sem.at[9], recv, (c, at_z(hop) * N_X + x))

    pass_on(0, 8, 4, z_sem.at[3])
    pass_on(0, 9, -4, z_sem.at[4])
    for j in range(1, 4):
        pass_on(0, 16 - 2 * j, j, z_sem.at[5])
        pass_on(0, 17 - 2 * j, -j, z_sem.at[5])

    osend[:, 0, :] = hidden
    orecv[block] = osend[mine_row]

    def send_row(k):
        to_x, to_core = lax.rem(x + k // 2, N_X), lax.rem(core + k, 2)
        to = (y * 2 + to_core, z * N_X + to_x)
        send(osend.at[to_core * N_X + to_x], orecv.at[block], send_sem.at[12], recv_sem.at[12], to)

    each(1, 8, send_row)
    track("row", orecv.at[pl.ds(0, 7)], 12)

    for side in range(2):
        drain(zbuf.at[8 + side], z_sem.at[3 + side])
        way = 1 - 2 * side

        @pl.when(z % 2 == side)
        def _():
            pass_on(8 + side, 1, 4 * way, recv_sem.at[9])

        for j in range(3):
            pass_on(8 + side, 2 + 2 * j + side, (3 - j) * way, recv_sem.at[9])
    sent.append((zbuf.at[pl.ds(0, N_Z - 1)], send_sem.at[9]))
    due["columns"] = (zbuf.at[pl.ds(0, 7)], recv_sem.at[9])
    drain(zbuf.at[pl.ds(10, 6)], z_sem.at[5])
    part = ROWS // 2
    near_rows = [
        dot(selection[g, :, part:], zbuf[8:, g].reshape(part, COLS)) for g in range(2)
    ]

    arrive("columns")
    for g in range(2):
        rows = dot(selection[g, :, :part], zbuf[:8, g].reshape(part, COLS))
        rows = (rows + near_rows[g]).astype(BF16)
        slots[g] = rows.reshape(N_X, 16, COLS)
        for i in range(1, N_X):
            to_x = lax.rem(x + i, N_X)
            to = (y * 2 + g, z * N_X + to_x)
            send(slots.at[g, to_x], gbuf.at[block], send_sem.at[10], recv_sem.at[10], to)
    to = (y * 2 + 1 - core, e)
    send(slots.at[1 - core, x], gbuf.at[block], send_sem.at[10], recv_sem.at[10], to)
    track("slots", gbuf.at[pl.ds(0, 7)], 10)
    gbuf[block] = slots[core, x]
    arrive("row")
    for i in range(8):
        hidden_ref[:, i * COLS : (i + 1) * COLS] = orecv[i].astype(BF16)
    arrive("slots")

    square = jnp.zeros((16, 1), F32)
    for i in range(8):
        rows = gbuf[i].astype(F32)
        square = square + jnp.sum(rows * rows, 1, keepdims=True)
    factor = lax.rsqrt(square * (1.0 / D) + 1e-06)
    for i in range(8):
        there = slice(i * COLS, (i + 1) * COLS)
        expert_ref[:, there] = (gbuf[i].astype(F32) * factor * gain[:, there]).astype(BF16)

    for ref, sem in sent:
        drain(ref, sem)


def place_results(hidden, expert_in, hidden_ref, expert_ref):
    hidden_ref[...] = hidden[...]
    for i in range(4):
        expert_ref[0, i] = expert_in[i * CAP : (i + 1) * CAP]


def on_device(
    prefill_cache,
    owner_slot,
    cached_len,
    query_latent,
    new_latent,
    wq_up,
    wk_up,
    wv_up,
    w_out,
    residual,
    ffn_gain,
    expert_ids,
):
    half = (10000.0 ** (-2.0 * np.arange(RD // 2, dtype=np.float32) / RD)).astype(np.float32)
    smem = pl.BlockSpec(memory_space=pltpu.SMEM)
    vmem = pl.BlockSpec(memory_space=pltpu.VMEM)
    anywhere = pl.BlockSpec(memory_space=pl.ANY)
    hidden, expert_in = pl.pallas_call(
        kernel,
        out_shape=(
            jax.ShapeDtypeStruct((1, D), BF16),
            jax.ShapeDtypeStruct((4 * CAP, D), BF16),
        ),
        in_specs=[smem] + [vmem] * 6 + [anywhere] * 7,
        out_specs=(vmem, vmem),
        scratch_shapes=[
            pltpu.VMEM((ROWS, QL), BF16),
            pltpu.VMEM((QW, QL), BF16),
            pltpu.VMEM((NOPE, KVL), BF16),
            pltpu.VMEM((KVL, VD), BF16),
            pltpu.VMEM((N_EXP, LLOC, RD), BF16),
            pltpu.VMEM((PAIRS, LLOC, 2 * RD), BF16),
            pltpu.VMEM((PAIRS, 2, LLOC, KVL), BF16),
            pltpu.VMEM((PAIRS, LLOC, 2 * RD), BF16),
            pltpu.VMEM((ROWS, LAT), BF16),
            pltpu.VMEM((N_CTX, SLOTS, QW), BF16),
            pltpu.VMEM((N_CTX, SLOTS, QW), BF16),
            pltpu.VMEM((N_CTX, SLOTS, LAT), BF16),
            pltpu.VMEM((N_CTX, SLOTS, LAT), BF16),
            pltpu.VMEM((PAIRS, 2, LAT), BF16),
            pltpu.VMEM((N_EXP, 2, LAT), BF16),
            pltpu.VMEM((N_EXP, 2, KVL + 128), BF16),
            pltpu.VMEM((N_EXP, 2, KVL + 128), BF16),
            pltpu.VMEM((N_CTX // 2, 2 * SLOTS, VD), BF16),
            pltpu.VMEM((N_CTX * N_X, 2 * SLOTS, VD), BF16),
            pltpu.VMEM((N_X, VD, COLS), BF16),
            pltpu.VMEM((N_Z, 8, COLS), BF16),
            pltpu.VMEM((2, 4, 8, COLS), BF16),
            pltpu.VMEM((2, 8, COLS), BF16),
            pltpu.VMEM((9, 8, COLS), BF16),
            pltpu.VMEM((8, 1, COLS), F32),
            pltpu.VMEM((8, 1, COLS), F32),
            pltpu.VMEM((TOPK, ROWS), jnp.int32),
            pltpu.VMEM((2, ROWS, ROWS), BF16),
            pltpu.VMEM((N_Z, 2, N_X, COLS), BF16),
            pltpu.VMEM((8, 1, COLS), F32),
            pltpu.VMEM((8, 1, COLS), F32),
            pltpu.VMEM((2, N_X, 16, COLS), BF16),
            pltpu.VMEM((8, 16, COLS), BF16),
            pltpu.SemaphoreType.DMA((6,)),
            pltpu.SemaphoreType.DMA((3,)),
            pltpu.SemaphoreType.DMA((14,)),
            pltpu.SemaphoreType.DMA((14,)),
            pltpu.SemaphoreType.DMA((6,)),
        ],
        compiler_params=pltpu.CompilerParams(
            collective_id=0, has_side_effects=True, vmem_limit_bytes=60 * 1024 * 1024
        ),
        cost_estimate=pl.CostEstimate(
            flops=600_000_000, bytes_accessed=8_000_000, transcendentals=40_000
        ),
    )(
        cached_len,
        owner_slot.reshape(1, N_CTX * ROWS),
        cached_len.reshape(1, N_CTX * ROWS),
        jnp.asarray(half).reshape(1, RD // 2),
        expert_ids.T,
        residual,
        ffn_gain.reshape(1, D),
        prefill_cache,
        query_latent,
        new_latent,
        wq_up.reshape(QL, QW).T,
        wk_up.reshape(NOPE, KVL),
        wv_up.reshape(KVL, VD),
        w_out,
    )
    return pl.pallas_call(
        place_results,
        out_shape=(
            jax.ShapeDtypeStruct((1, D), BF16),
            jax.ShapeDtypeStruct((1, 4, CAP, D), BF16),
        ),
        in_specs=[vmem] * 2,
        out_specs=(vmem, vmem),
    )(hidden, expert_in)


def solution(mesh):
    placed = (
        P("ctx", "exp", None),
        P(),
        P(),
        P("ctx", None),
        P("ctx", None),
        P(None, "exp", None),
        P("exp", None, None),
        P("exp", None, None),
        P("exp", None),
        P(("ctx", "exp"), None),
        P(),
        P("ctx", None),
    )
    return jax.shard_map(
        on_device,
        mesh=mesh,
        in_specs=placed,
        out_specs=(P(("ctx", "exp"), None), P("ctx", "exp", None, None)),
        check_vma=False,
    )
```
